32 devices in a mesh: tm: 8 (over z, y), state: 4 (over x, core).
Axes of the slice: x: 2, y: 2, z: 4, core: 2. Of those that a mesh axis runs over, the one named last changes fastest.
Arguments:
- dynamics: float32 [512, 512], P('state'), may hold values from -1 to 1
- pattern: int32 [4, 4], replicated, may hold values from 0 to 1
- initial_mean: float32 [4, 512], replicated, may hold values from -6 to 6
- observed: float32 [128, 4], P('tm'), may hold values from -6 to 6
- obs_index: int32 [128], P('tm'), may hold values from 0 to 511
- obs_noise: float32 [128], P('tm'), may hold values from 0.5 to 4
Outputs:
- filtered: float32 [128, 4, 512], P('tm', 'state')
- smoothed: float32 [128, 4, 512], P('tm', 'state')
The draws below stay inside these ranges and needn't reach their ends.
All inputs are finite; a program needn't handle non-finite values.
Results may differ from the reference program's by a relative error of at most 0.0003.
Values sent between devices are 32-bit elements; how exact they have to be, the bound alone decides.
A program may use at most 256 MiB of HBM per device.

```python
import math
import jax
import jax.numpy as jnp
from jax import lax

X = 512
NB = 4
B = 4
STEPS = 128


def draw_dynamics(key, part):
    first_key, second_key = jax.random.split(key, 2)
    rates = jnp.exp(jax.random.uniform(first_key, (X,), jnp.float32, math.log(1.0 / (2.0 * STEPS)), math.log(1.0 / 30.0)))
    raw_part = jnp.clip(jax.random.normal(second_key, (X, X), jnp.float32), -3.0, 3.0) * (0.035 / math.sqrt(X))
    decay = jnp.exp(-rates)
    skew_part = raw_part - raw_part.T
    return jnp.eye(X, dtype=jnp.float32) * decay[:, None] + skew_part


def draw_obs_index(key, part):
    first_key, second_key = jax.random.split(key, 2)
    base_index = jax.random.randint(first_key, (STEPS,), 0, X, jnp.int32)
    places = jax.random.permutation(second_key, STEPS)[:2]
    base_index = base_index.at[places[0]].set(0)
    return base_index.at[places[1]].set(X - 1)


def place_ends(values, key, least, high):
    longest = values.shape.index(max(values.shape))
    spots = []
    for shift in (0, 1):
        where = [jax.random.randint(jax.random.fold_in(key, axis), (), 0, length) for axis, length in enumerate(values.shape)]
        where[longest] = (where[longest] + shift) % values.shape[longest]
        spots.append(tuple(where))
    return values.at[spots[0]].set(least).at[spots[1]].set(high)


def level_of(key, shape, cuts, smallest, high):
    level = 1.0
    for axis_at, shards_of in cuts:
        draws = jax.random.uniform(jax.random.fold_in(jax.random.fold_in(key, 6), axis_at), (shards_of,), jnp.float32, smallest / len(cuts), high / len(cuts))
        level = level * jnp.repeat(jnp.exp(draws), shape[axis_at] // shards_of).reshape((-1,) + (1,) * (len(shape) - 1 - axis_at))
    return level


def noise(rng, extent, width, most, cuts=(), kind=jnp.bfloat16):
    entries = jax.random.normal(rng, extent, jnp.float32) * width
    if len(cuts) > 0:
        entries = level_of(rng, extent, cuts, -0.22, 0.18) * entries
    return jnp.clip(entries, min=-most, max=most).astype(kind)


def setup_inputs(seed: int = 0) -> dict:
    keys = jax.random.split(jax.random.key(seed), 7)
    return {
        "dynamics": draw_dynamics(jax.random.fold_in(keys[6], 71), 0),
        "pattern": place_ends(jax.random.randint(keys[1], (NB, NB), 0, 2), jax.random.fold_in(keys[1], 1), 0, 1).astype(jnp.int32),
        "initial_mean": noise(keys[2], (B, X), 1.0, 6.0, (), jnp.float32),
        "observed": noise(keys[3], (STEPS, B), 1.0, 6.0, ((0, 8),), jnp.float32),
        "obs_index": draw_obs_index(jax.random.fold_in(keys[6], 71), 0),
        "obs_noise": jnp.clip(jnp.exp(math.log(4.0) - 2.0794415 * jax.random.uniform(keys[5], (STEPS,), jnp.float32) ** level_of(keys[5], (STEPS,), ((0, 8),), -0.2, 0.2)), 0.5, 4.0),
    }


def product(left, right):
    return jnp.dot(left, right, precision=lax.Precision.HIGHEST, preferred_element_type=jnp.float32)


def reference(dynamics, pattern, initial_mean, observed, obs_index, obs_noise):
    blocks = pattern.shape[0]
    state_width = dynamics.shape[0]
    block_span = state_width // blocks
    present = jnp.maximum(pattern, jnp.eye(blocks, dtype=jnp.int32))
    block_mask = jnp.repeat(jnp.repeat(present, block_span, 0), block_span, 1).astype(jnp.float32)
    transition = dynamics * block_mask
    kalman_gains = 1.0 / (1.0 + obs_noise)
    state_index = jnp.arange(state_width, dtype=jnp.int32)
    observed_masks = (state_index[None, :] == obs_index[:, None]).astype(jnp.float32)
    scale_factors = 1.0 - kalman_gains[:, None] * observed_masks

    def filter_update(mean_now, inputs):
        scaling, hit_mask, gain_now, obs_now = inputs
        mean_now = product(mean_now, transition.T) * scaling[None, :] + gain_now * obs_now[:, None] * hit_mask[None, :]
        return mean_now, mean_now

    unused_value, filtered = lax.scan(filter_update, initial_mean, (scale_factors, observed_masks, kalman_gains, observed))
    retain_flags = jnp.ones((STEPS,), jnp.float32).at[STEPS - 1].set(0.0)

    def smoother_update(carried, inputs):
        mean_now, scaling, keep_flag = inputs
        gap_term = mean_now - keep_flag * product(product(mean_now, transition.T), transition) * scaling[None, :]
        carried = keep_flag * product(carried, transition) * scaling[None, :] + gap_term
        return carried, carried

    initial_zeros = jnp.zeros(initial_mean.shape, jnp.float32)
    unused_value, smoothed = lax.scan(smoother_update, initial_zeros, (filtered, scale_factors, retain_flags), reverse=True)
    return filtered, smoothed
```

```python
import functools

import jax
import jax.numpy as jnp
from jax import lax
from jax.experimental import pallas as pl
from jax.experimental.pallas import tpu as pltpu
from jax.sharding import PartitionSpec as P

MESH = pl.DeviceIdType.MESH
PIECES = 4
LANES = 128


def gather_kernel(members, segments, dyn_ref, packed_ref, full_ref, obs_ref,
                  x_send, x_recv, c_send, c_recv, f_send, f_recv, o_send, o_recv):
    me = lax.axis_index("state")
    seg = lax.axis_index("tm")
    rows = dyn_ref.shape[0]
    steps = packed_ref.shape[0]
    far = lax.rem(me + members // 2, members)
    near = me + 1 - 2 * lax.rem(me, 2)
    barrier = pltpu.get_barrier_semaphore()
    pl.semaphore_signal(barrier, inc=1, device_id={"state": far}, device_id_type=MESH)
    pl.semaphore_signal(barrier, inc=1, device_id={"state": near}, device_id_type=MESH)
    for d in range(1, segments):
        pl.semaphore_signal(barrier, inc=1, device_id={"tm": lax.rem(seg + d, segments)}, device_id_type=MESH)
    pl.semaphore_wait(barrier, segments + 1)

    piece = rows // PIECES
    own_start = pl.multiple_of(me * rows, rows)
    far_start = pl.multiple_of(far * rows, rows)
    copies = []
    crossing = []
    for i in range(PIECES):
        copy = pltpu.make_async_remote_copy(
            src_ref=dyn_ref.at[pl.ds(i * piece, piece)],
            dst_ref=full_ref.at[pl.ds(own_start + i * piece, piece)],
            send_sem=x_send.at[i], recv_sem=x_recv.at[i],
            device_id={"state": far}, device_id_type=MESH)
        copy.start()
        crossing.append(copy)
    for d in range(1, segments):
        copy = pltpu.make_async_remote_copy(
            src_ref=packed_ref,
            dst_ref=obs_ref.at[pl.ds(pl.multiple_of(seg * steps, steps), steps)],
            send_sem=o_send.at[d], recv_sem=o_recv.at[d],
            device_id={"tm": lax.rem(seg + d, segments)}, device_id_type=MESH)
        copy.start()
        copies.append(copy)
    copy = pltpu.make_async_remote_copy(
        src_ref=dyn_ref, dst_ref=full_ref.at[pl.ds(own_start, rows)],
        send_sem=c_send, recv_sem=c_recv,
        device_id={"state": near}, device_id_type=MESH)
    copy.start()
    copies.append(copy)
    full_ref[pl.ds(own_start, rows)] = dyn_ref[...]
    obs_ref[pl.ds(pl.multiple_of(seg * steps, steps), steps)] = packed_ref[...]
    for i in range(PIECES):
        crossing[i].wait_recv()
        spot = pl.ds(far_start + i * piece, piece)
        copy = pltpu.make_async_remote_copy(
            src_ref=full_ref.at[spot], dst_ref=full_ref.at[spot],
            send_sem=f_send.at[i], recv_sem=f_recv.at[i],
            device_id={"state": near}, device_id_type=MESH)
        copy.start()
        copies.append(copy)
    for copy in crossing:
        copy.wait_send()
    for copy in copies:
        copy.wait()


def halves(value):
    high = value.astype(jnp.bfloat16)
    low = (value - high.astype(jnp.float32)).astype(jnp.bfloat16)
    return high, low


def contract(left, right, dims):
    return lax.dot_general(left, right, (dims, ((), ())), preferred_element_type=jnp.float32)


def multiply(left, right, dims=((1,), (0,))):
    return (contract(left[0], right[1], dims) + contract(left[1], right[0], dims)) + contract(
        left[0], right[0], dims)


TRANS = ((1,), (1,))


def few_rows(left, right, dims=((1,), (0,))):
    count = left.shape[0]
    high = left.astype(jnp.bfloat16).astype(jnp.float32)
    both = jnp.concatenate([high, left - high], axis=0).astype(jnp.bfloat16)
    total = contract(both, right[1], dims) + contract(both, right[0], dims)
    return total[:count] + total[count:]


def compute_kernel(steps, full_ref, pattern_ref, mean_ref, obs_ref, filt_ref, smooth_ref,
                   power_hi, power_lo, powert_hi, powert_lo, r_hi, r_lo, p_hi, p_lo, h_hi, h_lo,
                   scaled_ref, obs_in_ref, hr_hi, hr_lo, u_ref, v_ref, x_ref, own_x, own_p):
    width = full_ref.shape[1]
    total = obs_ref.shape[0]
    blocks = pattern_ref.shape[0]
    span = width // blocks
    group = LANES
    groups = total // group
    chunks = total // steps
    per_group = group // steps
    levels = steps.bit_length() - 1
    sequences = mean_ref.shape[0]
    member = lax.axis_index("state")
    segment = lax.axis_index("tm")

    for i in range(blocks):
        for j in range(blocks):
            tile = full_ref[i * span:(i + 1) * span, j * span:(j + 1) * span]
            if i != j:
                tile = tile * jnp.maximum(pattern_ref[i, j], 0).astype(jnp.float32)
            hi, lo = halves(tile)
            power_hi[0, i * span:(i + 1) * span, j * span:(j + 1) * span] = hi
            power_lo[0, i * span:(i + 1) * span, j * span:(j + 1) * span] = lo

    for k in range(levels):
        square = multiply((power_hi[k], power_lo[k]), (power_hi[k], power_lo[k]))
        power_hi[k + 1], power_lo[k + 1] = halves(square)
    for k in range(levels + 1):
        powert_hi[k] = power_hi[k].T
        powert_lo[k] = power_lo[k].T

    row = lax.broadcasted_iota(jnp.int32, (group, group), 0)
    col = lax.broadcasted_iota(jnp.int32, (group, group), 1)
    wide = lax.broadcasted_iota(jnp.int32, (group, width), 1)
    row_wide = lax.broadcasted_iota(jnp.int32, (group, width), 0)

    def prepare(g):
        here = pl.ds(pl.multiple_of(g * group, group), group)
        packed = obs_ref[here, :]
        index = jnp.sum(jnp.where(col == sequences, packed, 0.0), axis=1, keepdims=True).astype(jnp.int32)
        noise = jnp.sum(jnp.where(col == sequences + 1, packed, 0.0), axis=1, keepdims=True)
        observed = jnp.sum(jnp.where(col == member, packed, 0.0), axis=1, keepdims=True)
        root = jnp.sqrt(1.0 / (1.0 + noise))
        scaled = jnp.where(wide == index, root, 0.0)
        scaled_ref[here, :] = scaled
        p_now = scaled
        r_now = multiply(halves(scaled), (power_hi[0], power_lo[0]))
        inverse = jnp.where(row == col, 1.0, 0.0)
        for k in range(levels):
            r_pair = halves(r_now)
            p_pair = halves(p_now)
            r_hi[k, here, :], r_lo[k, here, :] = r_pair
            p_hi[k, here, :], p_lo[k, here, :] = p_pair
            gram = multiply(r_pair, p_pair, TRANS)
            size = 2**k
            sibling = ((row // (2 * size)) == (col // (2 * size))) & ((row // size) == (col // size) + 1)
            gram = jnp.where(sibling, gram, 0.0)
            if k == 0:
                inverse = inverse - gram
            else:
                pair = halves(inverse)
                inverse = inverse - multiply(halves(multiply(pair, halves(gram))), pair)
            set_bit = ((row_wide // size) % 2) == 1
            r_now = jnp.where(set_bit, multiply(r_pair, (power_hi[k], power_lo[k])), r_now)
            p_now = jnp.where(set_bit, p_now, multiply(p_pair, (powert_hi[k], powert_lo[k])))
        r_pair = halves(r_now)
        r_hi[levels, here, :], r_lo[levels, here, :] = r_pair
        p_hi[levels, here, :], p_lo[levels, here, :] = halves(p_now)
        pair = halves(inverse)
        h_hi[here, :], h_lo[here, :] = pair
        hr_hi[here, :], hr_lo[here, :] = halves(multiply(pair, r_pair))
        source = multiply(pair, halves(jnp.where(col == member, observed * root, 0.0)))
        obs_in_ref[here, :] = jnp.broadcast_to(
            jnp.sum(source.T, axis=0, keepdims=True), (group, group))

    if groups == 1:
        prepare(0)
    else:
        lax.fori_loop(0, groups, lambda g, c: (prepare(g), c)[1], 0)

    lane8 = lax.broadcasted_iota(jnp.int32, (8, group), 1)
    u_ref[...] = jnp.zeros_like(u_ref)
    v_ref[...] = jnp.zeros_like(v_ref)
    top = (power_hi[levels], power_lo[levels])
    top_t = (powert_hi[levels], powert_lo[levels])

    def here_of(c):
        g = c // per_group
        return pl.ds(pl.multiple_of(g * group, group), group), pl.ds(pl.multiple_of(g * 8, 8), 8), c % per_group

    def forward(c, state):
        here, small, spot = here_of(c)
        x_ref[pl.ds(pl.multiple_of(c * 8, 8), 8), :] = state
        first = pl.ds(pl.multiple_of((c // per_group) * group, group), 8)
        drive = obs_in_ref[first, :] - few_rows(state, (hr_hi[here, :], hr_lo[here, :]), TRANS)
        drive = jnp.where(lane8 // steps == spot, drive, 0.0)
        u_ref[small, :] = u_ref[small, :] + drive
        return few_rows(state, top_t) + few_rows(drive, (p_hi[levels, here, :], p_lo[levels, here, :]))

    mean = jnp.sum(
        jnp.where(lax.broadcasted_iota(jnp.int32, mean_ref.shape, 0) == member, mean_ref[...], 0.0),
        axis=0, keepdims=True)
    state = jnp.broadcast_to(mean, (8, width))
    if chunks <= 8:
        for c in range(chunks):
            state = forward(c, state)
    else:
        state = lax.fori_loop(0, chunks, forward, state)
    x_ref[chunks * 8:(chunks + 1) * 8, :] = state

    def backward(i, state):
        c = chunks - 1 - i
        here, small, spot = here_of(c)
        own_p[pl.ds(pl.multiple_of(c * 8, 8), 8), :] = state
        seen = u_ref[small, :] - few_rows(state, (p_hi[levels, here, :], p_lo[levels, here, :]), TRANS)
        seen = jnp.where(lane8 // steps == spot, seen, 0.0)
        drive = few_rows(seen, (h_hi[here, :], h_lo[here, :]))
        drive = jnp.where(lane8 // steps == spot, drive, 0.0)
        v_ref[small, :] = v_ref[small, :] + drive
        return few_rows(state, top) + few_rows(drive, (r_hi[levels, here, :], r_lo[levels, here, :]))

    state = jnp.zeros((8, width), jnp.float32)
    if chunks <= 8:
        for i in range(chunks):
            state = backward(i, state)
    else:
        state = lax.fori_loop(0, chunks, backward, state)

    here, small, spot = here_of(segment)
    lane = lax.broadcasted_iota(jnp.int32, (steps, group), 1)
    tau = lax.broadcasted_iota(jnp.int32, (steps, group), 0)
    tall = lax.broadcasted_iota(jnp.int32, (steps, width), 0)
    local = lane - spot * steps
    mine = (local >= 0) & (local < steps)
    u_own = jnp.where(mine, jnp.broadcast_to(u_ref[small, :][:1], (steps, group)), 0.0)
    v_own = jnp.where(mine, jnp.broadcast_to(v_ref[small, :][:1], (steps, group)), 0.0)
    enter = x_ref[pl.ds(pl.multiple_of(segment * 8, 8), 8), :][:1]
    leave = x_ref[pl.ds(pl.multiple_of((segment + 1) * 8, 8), 8), :][:1]
    after = own_p[pl.ds(pl.multiple_of(segment * 8, 8), 8), :][:1]
    xs = jnp.where(tall == 0, jnp.broadcast_to(enter, (steps, width)), 0.0)
    ps = jnp.where(tall == steps - 1, jnp.broadcast_to(after, (steps, width)), 0.0)
    for k in reversed(range(levels)):
        size = 2**k
        u_use = jnp.where((local >= tau - size) & (local < tau), u_own, 0.0)
        v_use = jnp.where((local > tau) & (local <= tau + size), v_own, 0.0)
        p_level = (p_hi[k, here, :], p_lo[k, here, :])
        r_level = (r_hi[k, here, :], r_lo[k, here, :])
        moved = few_rows(pltpu.roll(xs, size, 0), (powert_hi[k], powert_lo[k])) + few_rows(u_use, p_level)
        xs = jnp.where(tall % (2 * size) == size, moved, xs)
        moved = few_rows(pltpu.roll(ps, steps - size, 0), (power_hi[k], power_lo[k])) + few_rows(v_use, r_level)
        ps = jnp.where((tall + 1) % (2 * size) == size, moved, ps)
    xs = jnp.where(tall == steps - 1, jnp.broadcast_to(leave, (steps, width)), pltpu.roll(xs, steps - 1, 0))
    hits = scaled_ref[pl.ds(pl.multiple_of(segment * steps, steps), steps), :]
    change = jnp.sum(jnp.where(local == tau, v_own - u_own, 0.0), axis=1, keepdims=True)
    filt_ref[...] = xs
    smooth_ref[...] = xs + ps + hits * change


def per_device(dynamics, pattern, initial_mean, observed, obs_index, obs_noise):
    rows, width = dynamics.shape
    sequences = initial_mean.shape[0]
    steps = observed.shape[0]
    members = lax.axis_size("state")
    segments = lax.axis_size("tm")
    total = steps * segments
    levels = steps.bit_length() - 1
    groups = total // LANES
    chunks = segments
    packed = jnp.concatenate(
        [observed, obs_index.astype(jnp.float32)[:, None], obs_noise[:, None],
         jnp.zeros((steps, LANES - sequences - 2), jnp.float32)], axis=1)
    vmem = pl.BlockSpec(memory_space=pltpu.VMEM)
    dma = pltpu.SemaphoreType.DMA
    full, gathered = pl.pallas_call(
        functools.partial(gather_kernel, members, segments),
        out_shape=(jax.ShapeDtypeStruct((rows * members, width), jnp.float32),
                   jax.ShapeDtypeStruct((total, LANES), jnp.float32)),
        in_specs=[vmem, vmem],
        out_specs=(vmem, vmem),
        scratch_shapes=[dma((PIECES,)), dma((PIECES,)), dma, dma, dma((PIECES,)), dma((PIECES,)),
                        dma((segments,)), dma((segments,))],
        compiler_params=pltpu.CompilerParams(collective_id=0, has_side_effects=True),
        name="gather",
    )(dynamics, packed)
    bf, f32 = jnp.bfloat16, jnp.float32
    out = jax.ShapeDtypeStruct((steps, width), f32)
    filtered, smoothed = pl.pallas_call(
        functools.partial(compute_kernel, steps),
        out_shape=(out, out),
        in_specs=[vmem, pl.BlockSpec(memory_space=pltpu.SMEM), vmem, vmem],
        out_specs=(vmem, vmem),
        scratch_shapes=(
            [pltpu.VMEM((levels + 1, width, width), bf)] * 4
            + [pltpu.VMEM((levels + 1, total, width), bf)] * 4
            + [pltpu.VMEM((total, LANES), bf)] * 2
            + [pltpu.VMEM((total, width), f32), pltpu.VMEM((total, LANES), f32)]
            + [pltpu.VMEM((total, width), bf)] * 2
            + [pltpu.VMEM((8 * groups, LANES), f32)] * 2
            + [pltpu.VMEM((8 * (chunks + 1), width), f32)] * 3),
        compiler_params=pltpu.CompilerParams(vmem_limit_bytes=56 * 1024 * 1024),
        name="smooth",
    )(full, pattern, initial_mean, gathered)
    return filtered[:, None, :], smoothed[:, None, :]


def solution(mesh):
    return jax.shard_map(
        per_device,
        mesh=mesh,
        in_specs=(P("state", None), P(), P(), P("tm", None), P("tm"), P("tm")),
        out_specs=(P("tm", "state", None), P("tm", "state", None)),
        check_vma=False,
    )
```

```python
import functools

import jax
import jax.numpy as jnp
from jax import lax
from jax.experimental import pallas as pl
from jax.experimental.pallas import tpu as pltpu
from jax.sharding import PartitionSpec as P

MESH = pl.DeviceIdType.MESH
PIECES = 4
LANES = 128


def gather_kernel(members, segments, dyn_ref, observed_ref, index_ref, noise_ref, full_ref, obs_ref,
                  raw_ref, packed_ref, x_send, x_recv, y_send, y_recv, c_send, c_recv,
                  f_send, f_recv, o_send, o_recv):
    me = lax.axis_index("state")
    seg = lax.axis_index("tm")
    rows = dyn_ref.shape[0]
    sequences, steps = observed_ref.shape
    far = lax.rem(me + members // 2, members)
    near = me + 1 - 2 * lax.rem(me, 2)
    side = lax.rem(seg, 2)
    across = seg + 1 - 2 * side
    barrier = pltpu.get_barrier_semaphore()
    pl.semaphore_signal(barrier, inc=1, device_id={"state": far}, device_id_type=MESH)
    pl.semaphore_signal(barrier, inc=1, device_id={"state": near}, device_id_type=MESH)
    for d in range(1, segments):
        pl.semaphore_signal(barrier, inc=1, device_id={"tm": lax.rem(seg + d, segments)}, device_id_type=MESH)
    raw_ref[...] = jnp.zeros_like(raw_ref)
    raw_ref[:sequences, :steps] = observed_ref[...]
    raw_ref[sequences:sequences + 1, :steps] = index_ref[...].astype(jnp.float32)
    raw_ref[sequences + 1:sequences + 2, :steps] = noise_ref[...]
    packed_ref[...] = raw_ref[...].T[:steps]
    pl.semaphore_wait(barrier, segments + 1)

    half = rows // 2
    piece = half // PIECES
    own_start = pl.multiple_of(me * rows, rows)
    far_start = pl.multiple_of(far * rows, rows)
    mine = side * half
    theirs = half - mine
    copies = []
    crossing = []
    swapping = []

    def send(src, dst, sends, recvs, target):
        copy = pltpu.make_async_remote_copy(
            src_ref=src, dst_ref=dst, send_sem=sends, recv_sem=recvs,
            device_id=target, device_id_type=MESH)
        copy.start()
        return copy

    for i in range(PIECES):
        at = pl.multiple_of(mine + i * piece, piece)
        crossing.append(send(dyn_ref.at[pl.ds(at, piece)],
                             full_ref.at[pl.ds(pl.multiple_of(own_start + at, piece), piece)],
                             x_send.at[i], x_recv.at[i], {"state": far}))
    for d in range(1, segments):
        copies.append(send(packed_ref, obs_ref.at[pl.ds(pl.multiple_of(seg * steps, steps), steps)],
                           o_send.at[d], o_recv.at[d], {"tm": lax.rem(seg + d, segments)}))
    copies.append(send(dyn_ref, full_ref.at[pl.ds(own_start, rows)], c_send, c_recv, {"state": near}))
    full_ref[pl.ds(own_start, rows)] = dyn_ref[...]
    obs_ref[pl.ds(pl.multiple_of(seg * steps, steps), steps)] = packed_ref[...]
    for i in range(PIECES):
        crossing[i].wait_recv()
        spot = pl.ds(pl.multiple_of(far_start + mine + i * piece, piece), piece)
        swapping.append(send(full_ref.at[spot], full_ref.at[spot], y_send.at[i], y_recv.at[i], {"tm": across}))
        copies.append(send(full_ref.at[spot], full_ref.at[spot], f_send.at[i], f_recv.at[i], {"state": near}))
    for i in range(PIECES):
        swapping[i].wait_recv()
        spot = pl.ds(pl.multiple_of(far_start + theirs + i * piece, piece), piece)
        copies.append(send(full_ref.at[spot], full_ref.at[spot], f_send.at[PIECES + i],
                           f_recv.at[PIECES + i], {"state": near}))
    for copy in crossing + swapping:
        copy.wait_send()
    for copy in copies:
        copy.wait()


def halves(value):
    high = value.astype(jnp.bfloat16)
    low = (value - high.astype(jnp.float32)).astype(jnp.bfloat16)
    return high, low


def contract(left, right, dims):
    return lax.dot_general(left, right, (dims, ((), ())), preferred_element_type=jnp.float32)


def multiply(left, right, dims=((1,), (0,))):
    return (contract(left[0], right[1], dims) + contract(left[1], right[0], dims)) + contract(
        left[0], right[0], dims)


TRANS = ((1,), (1,))


def few_rows(left, right, dims=((1,), (0,))):
    count = left.shape[0]
    high = left.astype(jnp.bfloat16).astype(jnp.float32)
    both = jnp.concatenate([high, left - high], axis=0).astype(jnp.bfloat16)
    total = contract(both, right[1], dims) + contract(both, right[0], dims)
    return total[:count] + total[count:]


def compute_kernel(steps, full_ref, pattern_ref, mean_ref, obs_ref, filt_ref, smooth_ref,
                   power_hi, power_lo, powert_hi, powert_lo, r_hi, r_lo, p_hi, p_lo, h_hi, h_lo,
                   scaled_ref, obs_in_ref, hr_hi, hr_lo, hrt_hi, hrt_lo, pt_hi, pt_lo, u_ref, v_ref, x_ref, own_x, own_p):
    width = full_ref.shape[1]
    total = obs_ref.shape[0]
    blocks = pattern_ref.shape[0]
    span = width // blocks
    group = LANES
    groups = total // group
    chunks = total // steps
    per_group = group // steps
    levels = steps.bit_length() - 1
    sequences = mean_ref.shape[0]
    member = lax.axis_index("state")
    segment = lax.axis_index("tm")

    for i in range(blocks):
        for j in range(blocks):
            tile = full_ref[i * span:(i + 1) * span, j * span:(j + 1) * span]
            if i != j:
                tile = tile * jnp.maximum(pattern_ref[i, j], 0).astype(jnp.float32)
            hi, lo = halves(tile)
            power_hi[0, i * span:(i + 1) * span, j * span:(j + 1) * span] = hi
            power_lo[0, i * span:(i + 1) * span, j * span:(j + 1) * span] = lo

    for k in range(levels):
        square = multiply((power_hi[k], power_lo[k]), (power_hi[k], power_lo[k]))
        power_hi[k + 1], power_lo[k + 1] = halves(square)
    for k in range(levels + 1):
        powert_hi[k] = power_hi[k].T
        powert_lo[k] = power_lo[k].T

    row = lax.broadcasted_iota(jnp.int32, (group, group), 0)
    col = lax.broadcasted_iota(jnp.int32, (group, group), 1)
    wide = lax.broadcasted_iota(jnp.int32, (group, width), 1)
    row_wide = lax.broadcasted_iota(jnp.int32, (group, width), 0)

    def prepare(g):
        here = pl.ds(pl.multiple_of(g * group, group), group)
        packed = obs_ref[here, :]
        index = jnp.sum(jnp.where(col == sequences, packed, 0.0), axis=1, keepdims=True).astype(jnp.int32)
        noise = jnp.sum(jnp.where(col == sequences + 1, packed, 0.0), axis=1, keepdims=True)
        observed = jnp.sum(jnp.where(col == member, packed, 0.0), axis=1, keepdims=True)
        root = jnp.sqrt(1.0 / (1.0 + noise))
        scaled = jnp.where(wide == index, root, 0.0)
        scaled_ref[here, :] = scaled
        p_now = scaled
        r_now = multiply(halves(scaled), (power_hi[0], power_lo[0]))
        inverse = jnp.where(row == col, 1.0, 0.0)
        for k in range(levels):
            r_pair = halves(r_now)
            p_pair = halves(p_now)
            r_hi[k, here, :], r_lo[k, here, :] = r_pair
            p_hi[k, here, :], p_lo[k, here, :] = p_pair
            gram = multiply(r_pair, p_pair, TRANS)
            size = 2**k
            sibling = ((row // (2 * size)) == (col // (2 * size))) & ((row // size) == (col // size) + 1)
            gram = jnp.where(sibling, gram, 0.0)
            if k == 0:
                inverse = inverse - gram
            else:
                pair = halves(inverse)
                inverse = inverse - multiply(halves(multiply(pair, halves(gram))), pair)
            set_bit = ((row_wide // size) % 2) == 1
            r_now = jnp.where(set_bit, multiply(r_pair, (power_hi[k], power_lo[k])), r_now)
            p_now = jnp.where(set_bit, p_now, multiply(p_pair, (powert_hi[k], powert_lo[k])))
        r_pair = halves(r_now)
        r_hi[levels, here, :], r_lo[levels, here, :] = r_pair
        p_hi[levels, here, :], p_lo[levels, here, :] = halves(p_now)
        tall_here = pl.ds(pl.multiple_of(g * width, width), width)
        pt_hi[tall_here, :], pt_lo[tall_here, :] = halves(p_now.T)
        pair = halves(inverse)
        h_hi[here, :], h_lo[here, :] = pair
        response = multiply(pair, r_pair)
        hr_hi[here, :], hr_lo[here, :] = halves(response)
        hrt_hi[tall_here, :], hrt_lo[tall_here, :] = halves(response.T)
        source = multiply(pair, halves(jnp.where(col == member, observed * root, 0.0)))
        obs_in_ref[here, :] = jnp.broadcast_to(
            jnp.sum(source.T, axis=0, keepdims=True), (group, group))

    if groups == 1:
        prepare(0)
    else:
        lax.fori_loop(0, groups, lambda g, c: (prepare(g), c)[1], 0)

    lane8 = lax.broadcasted_iota(jnp.int32, (8, group), 1)
    u_ref[...] = jnp.zeros_like(u_ref)
    v_ref[...] = jnp.zeros_like(v_ref)
    top = (power_hi[levels], power_lo[levels])
    top_t = (powert_hi[levels], powert_lo[levels])

    def here_of(c):
        g = c // per_group
        return pl.ds(pl.multiple_of(g * group, group), group), pl.ds(pl.multiple_of(g * 8, 8), 8), c % per_group

    def forward(c, state):
        here, small, spot = here_of(c)
        x_ref[pl.ds(pl.multiple_of(c * 8, 8), 8), :] = state
        first = pl.ds(pl.multiple_of((c // per_group) * group, group), 8)
        tall_here = pl.ds(pl.multiple_of((c // per_group) * width, width), width)
        drive = obs_in_ref[first, :] - few_rows(state, (hrt_hi[tall_here, :], hrt_lo[tall_here, :]))
        drive = jnp.where(lane8 // steps == spot, drive, 0.0)
        u_ref[small, :] = u_ref[small, :] + drive
        return few_rows(state, top_t) + few_rows(drive, (p_hi[levels, here, :], p_lo[levels, here, :]))

    mean = jnp.sum(
        jnp.where(lax.broadcasted_iota(jnp.int32, mean_ref.shape, 0) == member, mean_ref[...], 0.0),
        axis=0, keepdims=True)
    state = jnp.broadcast_to(mean, (8, width))
    if chunks <= 8:
        for c in range(chunks):
            state = forward(c, state)
    else:
        state = lax.fori_loop(0, chunks, forward, state)
    x_ref[chunks * 8:(chunks + 1) * 8, :] = state

    def backward(i, state):
        c = chunks - 1 - i
        here, small, spot = here_of(c)
        own_p[pl.ds(pl.multiple_of(c * 8, 8), 8), :] = state
        tall_here = pl.ds(pl.multiple_of((c // per_group) * width, width), width)
        seen = u_ref[small, :] - few_rows(state, (pt_hi[tall_here, :], pt_lo[tall_here, :]))
        seen = jnp.where(lane8 // steps == spot, seen, 0.0)
        v_ref[small, :] = v_ref[small, :] + seen
        return few_rows(state, top) + few_rows(seen, (hr_hi[here, :], hr_lo[here, :]))

    state = jnp.zeros((8, width), jnp.float32)
    if chunks <= 8:
        for i in range(chunks):
            state = backward(i, state)
    else:
        state = lax.fori_loop(0, chunks, backward, state)

    here, small, spot = here_of(segment)
    lane = lax.broadcasted_iota(jnp.int32, (steps, group), 1)
    tau = lax.broadcasted_iota(jnp.int32, (steps, group), 0)
    tall = lax.broadcasted_iota(jnp.int32, (steps, width), 0)
    local = lane - spot * steps
    mine = (local >= 0) & (local < steps)
    u_own = jnp.where(mine, jnp.broadcast_to(u_ref[small, :][:1], (steps, group)), 0.0)
    v_own = jnp.where(mine, jnp.broadcast_to(few_rows(v_ref[small, :], (h_hi[here, :], h_lo[here, :]))[:1], (steps, group)), 0.0)
    enter = x_ref[pl.ds(pl.multiple_of(segment * 8, 8), 8), :][:1]
    leave = x_ref[pl.ds(pl.multiple_of((segment + 1) * 8, 8), 8), :][:1]
    after = own_p[pl.ds(pl.multiple_of(segment * 8, 8), 8), :][:1]
    xs = jnp.where(tall == 0, jnp.broadcast_to(enter, (steps, width)), 0.0)
    ps = jnp.where(tall == steps - 1, jnp.broadcast_to(after, (steps, width)), 0.0)
    for k in reversed(range(levels)):
        size = 2**k
        u_use = jnp.where((local >= tau - size) & (local < tau), u_own, 0.0)
        v_use = jnp.where((local > tau) & (local <= tau + size), v_own, 0.0)
        p_level = (p_hi[k, here, :], p_lo[k, here, :])
        r_level = (r_hi[k, here, :], r_lo[k, here, :])
        moved = few_rows(pltpu.roll(xs, size, 0), (powert_hi[k], powert_lo[k])) + few_rows(u_use, p_level)
        xs = jnp.where(tall % (2 * size) == size, moved, xs)
        moved = few_rows(pltpu.roll(ps, steps - size, 0), (power_hi[k], power_lo[k])) + few_rows(v_use, r_level)
        ps = jnp.where((tall + 1) % (2 * size) == size, moved, ps)
    xs = jnp.where(tall == steps - 1, jnp.broadcast_to(leave, (steps, width)), pltpu.roll(xs, steps - 1, 0))
    hits = scaled_ref[pl.ds(pl.multiple_of(segment * steps, steps), steps), :]
    change = jnp.sum(jnp.where(local == tau, v_own - u_own, 0.0), axis=1, keepdims=True)
    ss = xs + ps + hits * change
    for i in range(steps):
        filt_ref[i] = xs[i:i + 1]
        smooth_ref[i] = ss[i:i + 1]


def per_device(dynamics, pattern, initial_mean, observed, obs_index, obs_noise):
    rows, width = dynamics.shape
    steps = observed.shape[0]
    members = lax.axis_size("state")
    segments = lax.axis_size("tm")
    total = steps * segments
    levels = steps.bit_length() - 1
    groups = total // LANES
    chunks = segments
    vmem = pl.BlockSpec(memory_space=pltpu.VMEM)
    dma = pltpu.SemaphoreType.DMA
    full, gathered = pl.pallas_call(
        functools.partial(gather_kernel, members, segments),
        out_shape=(jax.ShapeDtypeStruct((rows * members, width), jnp.float32),
                   jax.ShapeDtypeStruct((total, LANES), jnp.float32)),
        in_specs=[vmem] * 4,
        out_specs=(vmem, vmem),
        scratch_shapes=[pltpu.VMEM((LANES, LANES), jnp.float32), pltpu.VMEM((steps, LANES), jnp.float32),
                        dma((PIECES,)), dma((PIECES,)), dma((PIECES,)), dma((PIECES,)), dma, dma,
                        dma((2 * PIECES,)), dma((2 * PIECES,)),
                        dma((segments,)), dma((segments,))],
        compiler_params=pltpu.CompilerParams(collective_id=0, has_side_effects=True),
        name="gather",
    )(dynamics, observed.T, obs_index[None, :], obs_noise[None, :])
    bf, f32 = jnp.bfloat16, jnp.float32
    out = jax.ShapeDtypeStruct((steps, 1, width), f32)
    filtered, smoothed = pl.pallas_call(
        functools.partial(compute_kernel, steps),
        out_shape=(out, out),
        in_specs=[vmem, pl.BlockSpec(memory_space=pltpu.SMEM), vmem, vmem],
        out_specs=(vmem, vmem),
        scratch_shapes=(
            [pltpu.VMEM((levels + 1, width, width), bf)] * 4
            + [pltpu.VMEM((levels + 1, total, width), bf)] * 4
            + [pltpu.VMEM((total, LANES), bf)] * 2
            + [pltpu.VMEM((total, width), f32), pltpu.VMEM((total, LANES), f32)]
            + [pltpu.VMEM((total, width), bf)] * 2
            + [pltpu.VMEM((groups * width, LANES), bf)] * 4
            + [pltpu.VMEM((8 * groups, LANES), f32)] * 2
            + [pltpu.VMEM((8 * (chunks + 1), width), f32)] * 3),
        compiler_params=pltpu.CompilerParams(vmem_limit_bytes=56 * 1024 * 1024),
        name="smooth",
    )(full, pattern, initial_mean, gathered)
    return filtered, smoothed


def solution(mesh):
    return jax.shard_map(
        per_device,
        mesh=mesh,
        in_specs=(P("state", None), P(), P(), P("tm", None), P("tm"), P("tm")),
        out_specs=(P("tm", "state", None), P("tm", "state", None)),
        check_vma=False,
    )
```

```python
import functools

import jax
import jax.numpy as jnp
from jax import lax
from jax.experimental import pallas as pl
from jax.experimental.pallas import tpu as pltpu
from jax.sharding import PartitionSpec as P

MESH = pl.DeviceIdType.MESH
PIECES = 4
LANES = 128


def gather_kernel(members, segments, dyn_ref, observed_ref, index_ref, noise_ref, full_ref, obs_ref,
                  raw_ref, packed_ref, x_send, x_recv, y_send, y_recv, c_send, c_recv,
                  f_send, f_recv, o_send, o_recv, own_sem):
    me = lax.axis_index("state")
    seg = lax.axis_index("tm")
    rows = dyn_ref.shape[0]
    sequences, steps = observed_ref.shape
    far = lax.rem(me + members // 2, members)
    near = me + 1 - 2 * lax.rem(me, 2)
    side = lax.rem(seg, 2)
    across = seg + 1 - 2 * side
    barrier = pltpu.get_barrier_semaphore()
    pl.semaphore_signal(barrier, inc=1, device_id={"state": far}, device_id_type=MESH)
    pl.semaphore_signal(barrier, inc=1, device_id={"state": near}, device_id_type=MESH)
    for d in range(1, segments):
        pl.semaphore_signal(barrier, inc=1, device_id={"tm": lax.rem(seg + d, segments)}, device_id_type=MESH)
    raw_ref[...] = jnp.zeros_like(raw_ref)
    raw_ref[:sequences, :steps] = observed_ref[...]
    raw_ref[sequences:sequences + 1, :steps] = index_ref[...].astype(jnp.float32)
    raw_ref[sequences + 1:sequences + 2, :steps] = noise_ref[...]
    packed_ref[...] = raw_ref[...].T[:steps]
    pl.semaphore_wait(barrier, segments + 1)

    half = rows // 2
    piece = half // PIECES
    own_start = pl.multiple_of(me * rows, rows)
    far_start = pl.multiple_of(far * rows, rows)
    mine = side * half
    theirs = half - mine
    copies = []
    crossing = []
    swapping = []

    def send(src, dst, sends, recvs, target):
        copy = pltpu.make_async_remote_copy(
            src_ref=src, dst_ref=dst, send_sem=sends, recv_sem=recvs,
            device_id=target, device_id_type=MESH)
        copy.start()
        return copy

    for i in range(PIECES):
        at = pl.multiple_of(mine + i * piece, piece)
        crossing.append(send(dyn_ref.at[pl.ds(at, piece)],
                             full_ref.at[pl.ds(pl.multiple_of(own_start + at, piece), piece)],
                             x_send.at[i], x_recv.at[i], {"state": far}))
    for d in range(1, segments):
        copies.append(send(packed_ref, obs_ref.at[pl.ds(pl.multiple_of(seg * steps, steps), steps)],
                           o_send.at[d], o_recv.at[d], {"tm": lax.rem(seg + d, segments)}))
    copies.append(send(dyn_ref, full_ref.at[pl.ds(own_start, rows)], c_send, c_recv, {"state": near}))
    own_copy = pltpu.make_async_copy(dyn_ref, full_ref.at[pl.ds(own_start, rows)], own_sem)
    own_copy.start()
    obs_ref[pl.ds(pl.multiple_of(seg * steps, steps), steps)] = packed_ref[...]
    for i in range(PIECES):
        crossing[i].wait_recv()
        spot = pl.ds(pl.multiple_of(far_start + mine + i * piece, piece), piece)
        swapping.append(send(full_ref.at[spot], full_ref.at[spot], y_send.at[i], y_recv.at[i], {"tm": across}))
        copies.append(send(full_ref.at[spot], full_ref.at[spot], f_send.at[i], f_recv.at[i], {"state": near}))
    for i in range(PIECES):
        swapping[i].wait_recv()
        spot = pl.ds(pl.multiple_of(far_start + theirs + i * piece, piece), piece)
        copies.append(send(full_ref.at[spot], full_ref.at[spot], f_send.at[PIECES + i],
                           f_recv.at[PIECES + i], {"state": near}))
    own_copy.wait()
    for copy in crossing + swapping:
        copy.wait_send()
    for copy in copies:
        copy.wait()


def halves(value):
    high = value.astype(jnp.bfloat16)
    low = (value - high.astype(jnp.float32)).astype(jnp.bfloat16)
    return high, low


def contract(left, right, dims):
    return lax.dot_general(left, right, (dims, ((), ())), preferred_element_type=jnp.float32)


def multiply(left, right, dims=((1,), (0,))):
    stacked = jnp.concatenate([left[0], left[1], left[0]], axis=1)
    other = jnp.concatenate([right[1], right[0], right[0]], axis=dims[1][0])
    return contract(stacked, other, dims)


TRANS = ((1,), (1,))


def few_rows(left, right, dims=((1,), (0,))):
    count = left.shape[0]
    high = left.astype(jnp.bfloat16).astype(jnp.float32)
    both = jnp.concatenate([high, left - high], axis=0).astype(jnp.bfloat16)
    total = contract(jnp.concatenate([both, both], axis=1), jnp.concatenate([right[1], right[0]], axis=dims[1][0]), dims)
    return total[:count] + total[count:]


def compute_kernel(steps, full_ref, pattern_ref, mean_ref, obs_ref, filt_ref, smooth_ref,
                   power_hi, power_lo, powert_hi, powert_lo, r_hi, r_lo, p_hi, p_lo, h_hi, h_lo,
                   scaled_ref, obs_in_ref, hr_hi, hr_lo, hrt_hi, hrt_lo, pt_hi, pt_lo, u_ref, v_ref, x_ref, own_x, own_p):
    width = full_ref.shape[1]
    total = obs_ref.shape[0]
    blocks = pattern_ref.shape[0]
    span = width // blocks
    group = LANES
    groups = total // group
    chunks = total // steps
    per_group = group // steps
    levels = steps.bit_length() - 1
    sequences = mean_ref.shape[0]
    member = lax.axis_index("state")
    segment = lax.axis_index("tm")

    for i in range(blocks):
        for j in range(blocks):
            tile = full_ref[i * span:(i + 1) * span, j * span:(j + 1) * span]
            if i != j:
                tile = tile * jnp.maximum(pattern_ref[i, j], 0).astype(jnp.float32)
            down, over = slice(i * span, (i + 1) * span), slice(j * span, (j + 1) * span)
            power_hi[0, down, over], power_lo[0, down, over] = halves(tile)
            powert_hi[0, over, down], powert_lo[0, over, down] = halves(tile.T)

    def advance(k):
        square = multiply((power_hi[k], power_lo[k]), (power_hi[k], power_lo[k]))
        power_hi[k + 1], power_lo[k + 1] = halves(square)
        powert_hi[k + 1], powert_lo[k + 1] = halves(square.T)

    if groups > 1:
        for k in range(levels):
            advance(k)

    row = lax.broadcasted_iota(jnp.int32, (group, group), 0)
    col = lax.broadcasted_iota(jnp.int32, (group, group), 1)
    wide = lax.broadcasted_iota(jnp.int32, (group, width), 1)
    row_wide = lax.broadcasted_iota(jnp.int32, (group, width), 0)

    def prepare(g):
        here = pl.ds(pl.multiple_of(g * group, group), group)
        packed = obs_ref[here, :]
        index = jnp.sum(jnp.where(col == sequences, packed, 0.0), axis=1, keepdims=True).astype(jnp.int32)
        noise = jnp.sum(jnp.where(col == sequences + 1, packed, 0.0), axis=1, keepdims=True)
        observed = jnp.sum(jnp.where(col == member, packed, 0.0), axis=1, keepdims=True)
        root = jnp.sqrt(1.0 / (1.0 + noise))
        scaled = jnp.where(wide == index, root, 0.0)
        scaled_ref[here, :] = scaled
        p_now = scaled
        r_now = multiply(halves(scaled), (power_hi[0], power_lo[0]))
        inverse = jnp.where(row == col, 1.0, 0.0)
        for k in range(levels):
            if groups == 1:
                advance(k)
            r_pair = halves(r_now)
            p_pair = halves(p_now)
            r_hi[k, here, :], r_lo[k, here, :] = r_pair
            p_hi[k, here, :], p_lo[k, here, :] = p_pair
            gram = multiply(r_pair, p_pair, TRANS)
            size = 2**k
            sibling = ((row // (2 * size)) == (col // (2 * size))) & ((row // size) == (col // size) + 1)
            gram = jnp.where(sibling, gram, 0.0)
            if k == 0:
                inverse = inverse - gram
            else:
                pair = halves(inverse)
                inverse = inverse - multiply(halves(multiply(pair, halves(gram))), pair)
            set_bit = ((row_wide // size) % 2) == 1
            r_now = jnp.where(set_bit, multiply(r_pair, (power_hi[k], power_lo[k])), r_now)
            p_now = jnp.where(set_bit, p_now, multiply(p_pair, (powert_hi[k], powert_lo[k])))
        r_pair = halves(r_now)
        r_hi[levels, here, :], r_lo[levels, here, :] = r_pair
        p_hi[levels, here, :], p_lo[levels, here, :] = halves(p_now)
        tall_here = pl.ds(pl.multiple_of(g * width, width), width)
        pt_hi[tall_here, :], pt_lo[tall_here, :] = halves(p_now.T)
        pair = halves(inverse)
        h_hi[here, :], h_lo[here, :] = pair
        response = multiply(pair, r_pair)
        hr_hi[here, :], hr_lo[here, :] = halves(response)
        hrt_hi[tall_here, :], hrt_lo[tall_here, :] = halves(response.T)
        source = multiply(pair, halves(jnp.where(col == member, observed * root, 0.0)))
        obs_in_ref[here, :] = jnp.broadcast_to(
            jnp.sum(source.T, axis=0, keepdims=True), (group, group))

    if groups == 1:
        prepare(0)
    else:
        lax.fori_loop(0, groups, lambda g, c: (prepare(g), c)[1], 0)

    lane8 = lax.broadcasted_iota(jnp.int32, (8, group), 1)
    u_ref[...] = jnp.zeros_like(u_ref)
    v_ref[...] = jnp.zeros_like(v_ref)
    top = (power_hi[levels], power_lo[levels])
    top_t = (powert_hi[levels], powert_lo[levels])

    def here_of(c):
        g = c // per_group
        return pl.ds(pl.multiple_of(g * group, group), group), pl.ds(pl.multiple_of(g * 8, 8), 8), c % per_group

    def forward(c, state):
        here, small, spot = here_of(c)
        x_ref[pl.ds(pl.multiple_of(c * 8, 8), 8), :] = state
        first = pl.ds(pl.multiple_of((c // per_group) * group, group), 8)
        tall_here = pl.ds(pl.multiple_of((c // per_group) * width, width), width)
        drive = obs_in_ref[first, :] - few_rows(state, (hrt_hi[tall_here, :], hrt_lo[tall_here, :]))
        drive = jnp.where(lane8 // steps == spot, drive, 0.0)
        u_ref[small, :] = u_ref[small, :] + drive
        return few_rows(state, top_t) + few_rows(drive, (p_hi[levels, here, :], p_lo[levels, here, :]))

    mean = jnp.sum(
        jnp.where(lax.broadcasted_iota(jnp.int32, mean_ref.shape, 0) == member, mean_ref[...], 0.0),
        axis=0, keepdims=True)
    state = jnp.broadcast_to(mean, (8, width))
    if chunks <= 8:
        for c in range(chunks):
            state = forward(c, state)
    else:
        state = lax.fori_loop(0, chunks, forward, state)
    x_ref[chunks * 8:(chunks + 1) * 8, :] = state

    def backward(i, state):
        c = chunks - 1 - i
        here, small, spot = here_of(c)
        own_p[pl.ds(pl.multiple_of(c * 8, 8), 8), :] = state
        tall_here = pl.ds(pl.multiple_of((c // per_group) * width, width), width)
        seen = u_ref[small, :] - few_rows(state, (pt_hi[tall_here, :], pt_lo[tall_here, :]))
        seen = jnp.where(lane8 // steps == spot, seen, 0.0)
        v_ref[small, :] = v_ref[small, :] + seen
        return few_rows(state, top) + few_rows(seen, (hr_hi[here, :], hr_lo[here, :]))

    here, small, spot = here_of(segment)
    lane = lax.broadcasted_iota(jnp.int32, (steps, group), 1)
    tau = lax.broadcasted_iota(jnp.int32, (steps, group), 0)
    tall = lax.broadcasted_iota(jnp.int32, (steps, width), 0)
    local = lane - spot * steps
    mine = (local >= 0) & (local < steps)
    u_own = jnp.where(mine, jnp.broadcast_to(u_ref[small, :][:1], (steps, group)), 0.0)
    enter = x_ref[pl.ds(pl.multiple_of(segment * 8, 8), 8), :][:1]
    leave = x_ref[pl.ds(pl.multiple_of((segment + 1) * 8, 8), 8), :][:1]
    first_xs = jnp.where(tall == 0, jnp.broadcast_to(enter, (steps, width)), 0.0)

    def expand(k, xs):
        size = 2**k
        u_use = jnp.where((local >= tau - size) & (local < tau), u_own, 0.0)
        moved = few_rows(pltpu.roll(xs, size, 0), (powert_hi[k], powert_lo[k])) + few_rows(
            u_use, (p_hi[k, here, :], p_lo[k, here, :]))
        return jnp.where(tall % (2 * size) == size, moved, xs)

    state = jnp.zeros((8, width), jnp.float32)
    xs = first_xs
    if chunks <= 8:
        for i in range(chunks):
            state = backward(i, state)
            if i < levels:
                xs = expand(levels - 1 - i, xs)
        done = min(chunks, levels)
    else:
        state = lax.fori_loop(0, chunks, backward, state)
        done = 0
    for i in range(done, levels):
        xs = expand(levels - 1 - i, xs)
    xs = jnp.where(tall == steps - 1, jnp.broadcast_to(leave, (steps, width)), pltpu.roll(xs, steps - 1, 0))

    v_all = few_rows(v_ref[small, :], (h_hi[here, :], h_lo[here, :]))
    v_own = jnp.where(mine, jnp.broadcast_to(v_all[:1], (steps, group)), 0.0)
    after = own_p[pl.ds(pl.multiple_of(segment * 8, 8), 8), :][:1]
    ps = jnp.where(tall == steps - 1, jnp.broadcast_to(after, (steps, width)), 0.0)
    for k in reversed(range(levels)):
        size = 2**k
        v_use = jnp.where((local > tau) & (local <= tau + size), v_own, 0.0)
        moved = few_rows(pltpu.roll(ps, steps - size, 0), (power_hi[k], power_lo[k])) + few_rows(
            v_use, (r_hi[k, here, :], r_lo[k, here, :]))
        ps = jnp.where((tall + 1) % (2 * size) == size, moved, ps)
    hits = scaled_ref[pl.ds(pl.multiple_of(segment * steps, steps), steps), :]
    change = jnp.sum(jnp.where(local == tau, v_own - u_own, 0.0), axis=1, keepdims=True)
    ss = xs + ps + hits * change
    for i in range(steps):
        filt_ref[i] = xs[i:i + 1]
        smooth_ref[i] = ss[i:i + 1]


def per_device(dynamics, pattern, initial_mean, observed, obs_index, obs_noise):
    rows, width = dynamics.shape
    steps = observed.shape[0]
    members = lax.axis_size("state")
    segments = lax.axis_size("tm")
    total = steps * segments
    levels = steps.bit_length() - 1
    groups = total // LANES
    chunks = segments
    vmem = pl.BlockSpec(memory_space=pltpu.VMEM)
    hbm = pl.BlockSpec(memory_space=pl.ANY)
    dma = pltpu.SemaphoreType.DMA
    full, gathered = pl.pallas_call(
        functools.partial(gather_kernel, members, segments),
        out_shape=(jax.ShapeDtypeStruct((rows * members, width), jnp.float32),
                   jax.ShapeDtypeStruct((total, LANES), jnp.float32)),
        in_specs=[hbm, vmem, vmem, vmem],
        out_specs=(hbm, vmem),
        scratch_shapes=[pltpu.VMEM((LANES, LANES), jnp.float32), pltpu.VMEM((steps, LANES), jnp.float32),
                        dma((PIECES,)), dma((PIECES,)), dma((PIECES,)), dma((PIECES,)), dma, dma,
                        dma((2 * PIECES,)), dma((2 * PIECES,)),
                        dma((segments,)), dma((segments,)), dma],
        compiler_params=pltpu.CompilerParams(collective_id=0, has_side_effects=True),
        name="gather",
    )(dynamics, observed.T, obs_index[None, :], obs_noise[None, :])
    bf, f32 = jnp.bfloat16, jnp.float32
    out = jax.ShapeDtypeStruct((steps, 1, width), f32)
    filtered, smoothed = pl.pallas_call(
        functools.partial(compute_kernel, steps),
        out_shape=(out, out),
        in_specs=[vmem, pl.BlockSpec(memory_space=pltpu.SMEM), vmem, vmem],
        out_specs=(vmem, vmem),
        scratch_shapes=(
            [pltpu.VMEM((levels + 1, width, width), bf)] * 4
            + [pltpu.VMEM((levels + 1, total, width), bf)] * 4
            + [pltpu.VMEM((total, LANES), bf)] * 2
            + [pltpu.VMEM((total, width), f32), pltpu.VMEM((total, LANES), f32)]
            + [pltpu.VMEM((total, width), bf)] * 2
            + [pltpu.VMEM((groups * width, LANES), bf)] * 4
            + [pltpu.VMEM((8 * groups, LANES), f32)] * 2
            + [pltpu.VMEM((8 * (chunks + 1), width), f32)] * 3),
        compiler_params=pltpu.CompilerParams(vmem_limit_bytes=56 * 1024 * 1024),
        name="smooth",
    )(full, pattern, initial_mean, gathered)
    return filtered, smoothed


def solution(mesh):
    return jax.shard_map(
        per_device,
        mesh=mesh,
        in_specs=(P("state", None), P(), P(), P("tm", None), P("tm"), P("tm")),
        out_specs=(P("tm", "state", None), P("tm", "state", None)),
        check_vma=False,
    )
```

```python
import functools

import jax
import jax.numpy as jnp
from jax import lax
from jax.experimental import pallas as pl
from jax.experimental.pallas import tpu as pltpu
from jax.sharding import PartitionSpec as P

MESH = pl.DeviceIdType.MESH
PIECES = 4
LANES = 128


def gather_kernel(members, segments, dyn_ref, observed_ref, index_ref, noise_ref, full_ref, obs_ref,
                  raw_ref, packed_ref, x_send, x_recv, y_send, y_recv, c_send, c_recv,
                  f_send, f_recv, o_send, o_recv, own_sem):
    me = lax.axis_index("state")
    seg = lax.axis_index("tm")
    rows = dyn_ref.shape[0]
    sequences, steps = observed_ref.shape
    far = lax.rem(me + members // 2, members)
    near = me + 1 - 2 * lax.rem(me, 2)
    side = lax.rem(seg, 2)
    across = seg + 1 - 2 * side
    barrier = pltpu.get_barrier_semaphore()
    pl.semaphore_signal(barrier, inc=1, device_id={"state": far}, device_id_type=MESH)
    pl.semaphore_signal(barrier, inc=1, device_id={"state": near}, device_id_type=MESH)
    for d in range(1, segments):
        pl.semaphore_signal(barrier, inc=1, device_id={"tm": lax.rem(seg + d, segments)}, device_id_type=MESH)
    pl.semaphore_wait(barrier, segments + 1)

    half = rows // 2
    piece = half // PIECES
    own_start = pl.multiple_of(me * rows, rows)
    far_start = pl.multiple_of(far * rows, rows)
    mine = side * half
    theirs = half - mine
    copies = []
    crossing = []
    swapping = []

    def send(src, dst, sends, recvs, target):
        copy = pltpu.make_async_remote_copy(
            src_ref=src, dst_ref=dst, send_sem=sends, recv_sem=recvs,
            device_id=target, device_id_type=MESH)
        copy.start()
        return copy

    for i in range(PIECES):
        at = pl.multiple_of(mine + i * piece, piece)
        crossing.append(send(dyn_ref.at[pl.ds(at, piece)],
                             full_ref.at[pl.ds(pl.multiple_of(own_start + at, piece), piece)],
                             x_send.at[i], x_recv.at[i], {"state": far}))
    copies.append(send(dyn_ref, full_ref.at[pl.ds(own_start, rows)], c_send, c_recv, {"state": near}))
    raw_ref[...] = jnp.zeros_like(raw_ref)
    raw_ref[:sequences, :steps] = observed_ref[...]
    raw_ref[sequences:sequences + 1, :steps] = index_ref[...].astype(jnp.float32)
    raw_ref[sequences + 1:sequences + 2, :steps] = noise_ref[...]
    packed_ref[...] = raw_ref[...].T[:steps]
    for d in range(1, segments):
        copies.append(send(packed_ref, obs_ref.at[pl.ds(pl.multiple_of(seg * steps, steps), steps)],
                           o_send.at[d], o_recv.at[d], {"tm": lax.rem(seg + d, segments)}))
    own_copy = pltpu.make_async_copy(dyn_ref, full_ref.at[pl.ds(own_start, rows)], own_sem)
    own_copy.start()
    obs_ref[pl.ds(pl.multiple_of(seg * steps, steps), steps)] = packed_ref[...]
    for i in range(PIECES):
        crossing[i].wait_recv()
        spot = pl.ds(pl.multiple_of(far_start + mine + i * piece, piece), piece)
        swapping.append(send(full_ref.at[spot], full_ref.at[spot], y_send.at[i], y_recv.at[i], {"tm": across}))
        copies.append(send(full_ref.at[spot], full_ref.at[spot], f_send.at[i], f_recv.at[i], {"state": near}))
    for i in range(PIECES):
        swapping[i].wait_recv()
        spot = pl.ds(pl.multiple_of(far_start + theirs + i * piece, piece), piece)
        copies.append(send(full_ref.at[spot], full_ref.at[spot], f_send.at[PIECES + i],
                           f_recv.at[PIECES + i], {"state": near}))
    own_copy.wait()
    for copy in crossing + swapping:
        copy.wait_send()
    for copy in copies:
        copy.wait()


def halves(value):
    high = value.astype(jnp.bfloat16)
    low = (value - high.astype(jnp.float32)).astype(jnp.bfloat16)
    return high, low


def contract(left, right, dims):
    return lax.dot_general(left, right, (dims, ((), ())), preferred_element_type=jnp.float32)


def multiply(left, right, dims=((1,), (0,))):
    stacked = jnp.concatenate([left[0], left[1], left[0]], axis=1)
    other = jnp.concatenate([right[1], right[0], right[0]], axis=dims[1][0])
    return contract(stacked, other, dims)


TRANS = ((1,), (1,))


def few_rows(left, right, dims=((1,), (0,))):
    count = left.shape[0]
    high = left.astype(jnp.bfloat16).astype(jnp.float32)
    both = jnp.concatenate([high, left - high], axis=0).astype(jnp.bfloat16)
    total = contract(jnp.concatenate([both, both], axis=1), jnp.concatenate([right[1], right[0]], axis=dims[1][0]), dims)
    return total[:count] + total[count:]


def compute_kernel(steps, full_ref, pattern_ref, mean_ref, obs_ref, filt_ref, smooth_ref,
                   power_hi, power_lo, powert_hi, powert_lo, r_hi, r_lo, p_hi, p_lo, h_hi, h_lo,
                   scaled_ref, obs_in_ref, hr_hi, hr_lo, hrt_hi, hrt_lo, pt_hi, pt_lo, th_hi, th_lo, tp_hi, tp_lo, kt_hi, kt_lo, kb_hi, kb_lo, u_ref, v_ref, x_ref, own_x, own_p):
    width = full_ref.shape[1]
    total = obs_ref.shape[0]
    blocks = pattern_ref.shape[0]
    span = width // blocks
    group = LANES
    groups = total // group
    chunks = total // steps
    per_group = group // steps
    levels = steps.bit_length() - 1
    sequences = mean_ref.shape[0]
    member = lax.axis_index("state")
    segment = lax.axis_index("tm")

    for i in range(blocks):
        for j in range(blocks):
            tile = full_ref[i * span:(i + 1) * span, j * span:(j + 1) * span]
            if i != j:
                tile = tile * jnp.maximum(pattern_ref[i, j], 0).astype(jnp.float32)
            down, over = slice(i * span, (i + 1) * span), slice(j * span, (j + 1) * span)
            power_hi[0, down, over], power_lo[0, down, over] = halves(tile)
            powert_hi[0, over, down], powert_lo[0, over, down] = halves(tile.T)

    def advance(k):
        square = multiply((power_hi[k], power_lo[k]), (power_hi[k], power_lo[k]))
        power_hi[k + 1], power_lo[k + 1] = halves(square)
        powert_hi[k + 1], powert_lo[k + 1] = halves(square.T)

    if groups > 1:
        for k in range(levels):
            advance(k)

    row = lax.broadcasted_iota(jnp.int32, (group, group), 0)
    col = lax.broadcasted_iota(jnp.int32, (group, group), 1)
    wide = lax.broadcasted_iota(jnp.int32, (group, width), 1)
    row_wide = lax.broadcasted_iota(jnp.int32, (group, width), 0)

    def prepare(g):
        here = pl.ds(pl.multiple_of(g * group, group), group)
        packed = obs_ref[here, :]
        index = jnp.sum(jnp.where(col == sequences, packed, 0.0), axis=1, keepdims=True).astype(jnp.int32)
        noise = jnp.sum(jnp.where(col == sequences + 1, packed, 0.0), axis=1, keepdims=True)
        observed = jnp.sum(jnp.where(col == member, packed, 0.0), axis=1, keepdims=True)
        root = jnp.sqrt(1.0 / (1.0 + noise))
        scaled = jnp.where(wide == index, root, 0.0)
        scaled_ref[here, :] = scaled
        p_now = scaled
        r_now = multiply(halves(scaled), (power_hi[0], power_lo[0]))
        inverse = jnp.where(row == col, 1.0, 0.0)
        for k in range(levels):
            if groups == 1:
                advance(k)
            r_pair = halves(r_now)
            p_pair = halves(p_now)
            r_hi[k, here, :], r_lo[k, here, :] = r_pair
            p_hi[k, here, :], p_lo[k, here, :] = p_pair
            gram = multiply(r_pair, p_pair, TRANS)
            size = 2**k
            sibling = ((row // (2 * size)) == (col // (2 * size))) & ((row // size) == (col // size) + 1)
            gram = jnp.where(sibling, gram, 0.0)
            if k == 0:
                inverse = inverse - gram
            else:
                pair = halves(inverse)
                inverse = inverse - multiply(halves(multiply(pair, halves(gram))), pair)
            set_bit = ((row_wide // size) % 2) == 1
            r_now = jnp.where(set_bit, multiply(r_pair, (power_hi[k], power_lo[k])), r_now)
            p_now = jnp.where(set_bit, p_now, multiply(p_pair, (powert_hi[k], powert_lo[k])))
        r_pair = halves(r_now)
        r_hi[levels, here, :], r_lo[levels, here, :] = r_pair
        p_hi[levels, here, :], p_lo[levels, here, :] = halves(p_now)
        tall_here = pl.ds(pl.multiple_of(g * width, width), width)
        pt_hi[tall_here, :], pt_lo[tall_here, :] = halves(p_now.T)
        pair = halves(inverse)
        h_hi[here, :], h_lo[here, :] = pair
        response = multiply(pair, r_pair)
        hr_hi[here, :], hr_lo[here, :] = halves(response)
        hrt_hi[tall_here, :], hrt_lo[tall_here, :] = halves(response.T)
        if groups == 1:
            p_pair = halves(p_now)
            response_pair = halves(response)
            th_hi[...], th_lo[...] = halves(
                multiply(response_pair, (power_hi[levels], power_lo[levels])).T)
            tp_hi[...], tp_lo[...] = halves(
                multiply(p_pair, (powert_hi[levels], powert_lo[levels])).T)
            link = multiply(p_pair, response_pair, TRANS)
            kt_hi[...], kt_lo[...] = halves(link)
            kb_hi[...], kb_lo[...] = halves(link.T)
        source = multiply(pair, halves(jnp.where(col == member, observed * root, 0.0)))
        obs_in_ref[here, :] = jnp.broadcast_to(
            jnp.sum(source.T, axis=0, keepdims=True), (group, group))

    if groups == 1:
        prepare(0)
    else:
        lax.fori_loop(0, groups, lambda g, c: (prepare(g), c)[1], 0)

    lane8 = lax.broadcasted_iota(jnp.int32, (8, group), 1)
    u_ref[...] = jnp.zeros_like(u_ref)
    v_ref[...] = jnp.zeros_like(v_ref)
    top = (power_hi[levels], power_lo[levels])
    top_t = (powert_hi[levels], powert_lo[levels])

    def here_of(c):
        g = c // per_group
        return pl.ds(pl.multiple_of(g * group, group), group), pl.ds(pl.multiple_of(g * 8, 8), 8), c % per_group

    def forward(c, state):
        here, small, spot = here_of(c)
        x_ref[pl.ds(pl.multiple_of(c * 8, 8), 8), :] = state
        first = pl.ds(pl.multiple_of((c // per_group) * group, group), 8)
        tall_here = pl.ds(pl.multiple_of((c // per_group) * width, width), width)
        drive = obs_in_ref[first, :] - few_rows(state, (hrt_hi[tall_here, :], hrt_lo[tall_here, :]))
        drive = jnp.where(lane8 // steps == spot, drive, 0.0)
        u_ref[small, :] = u_ref[small, :] + drive
        return few_rows(state, top_t) + few_rows(drive, (p_hi[levels, here, :], p_lo[levels, here, :]))

    mean = jnp.sum(
        jnp.where(lax.broadcasted_iota(jnp.int32, mean_ref.shape, 0) == member, mean_ref[...], 0.0),
        axis=0, keepdims=True)
    state = jnp.broadcast_to(mean, (8, width))
    ahead = groups == 1 and chunks <= 8
    if ahead:
        th, tp = (th_hi[...], th_lo[...]), (tp_hi[...], tp_lo[...])
        kt, kb = (kt_hi[...], kt_lo[...]), (kb_hi[...], kb_lo[...])
        base = obs_in_ref[:8, :]
        shown = few_rows(state, (hrt_hi[...], hrt_lo[...]))
        every = jnp.zeros((8, group), jnp.float32)
        for c in range(chunks):
            x_ref[c * 8:(c + 1) * 8, :] = state
            drive = jnp.where(lane8 // steps == c, base - shown, 0.0)
            every = every + drive
            if c + 1 < chunks:
                shown = few_rows(state, th) + few_rows(drive, kt)
            state = few_rows(state, top_t) + few_rows(drive, (p_hi[levels], p_lo[levels]))
        u_ref[...] = every
    else:
        state = lax.fori_loop(0, chunks, forward, state)
    x_ref[chunks * 8:(chunks + 1) * 8, :] = state

    def backward(i, state):
        c = chunks - 1 - i
        here, small, spot = here_of(c)
        own_p[pl.ds(pl.multiple_of(c * 8, 8), 8), :] = state
        tall_here = pl.ds(pl.multiple_of((c // per_group) * width, width), width)
        seen = u_ref[small, :] - few_rows(state, (pt_hi[tall_here, :], pt_lo[tall_here, :]))
        seen = jnp.where(lane8 // steps == spot, seen, 0.0)
        v_ref[small, :] = v_ref[small, :] + seen
        return few_rows(state, top) + few_rows(seen, (hr_hi[here, :], hr_lo[here, :]))

    here, small, spot = here_of(segment)
    lane = lax.broadcasted_iota(jnp.int32, (steps, group), 1)
    tau = lax.broadcasted_iota(jnp.int32, (steps, group), 0)
    tall = lax.broadcasted_iota(jnp.int32, (steps, width), 0)
    local = lane - spot * steps
    mine = (local >= 0) & (local < steps)
    u_own = jnp.where(mine, jnp.broadcast_to(u_ref[small, :][:1], (steps, group)), 0.0)
    enter = x_ref[pl.ds(pl.multiple_of(segment * 8, 8), 8), :][:1]
    leave = x_ref[pl.ds(pl.multiple_of((segment + 1) * 8, 8), 8), :][:1]
    first_xs = jnp.where(tall == 0, jnp.broadcast_to(enter, (steps, width)), 0.0)

    def expand(k, xs):
        size = 2**k
        u_use = jnp.where((local >= tau - size) & (local < tau), u_own, 0.0)
        moved = few_rows(pltpu.roll(xs, size, 0), (powert_hi[k], powert_lo[k])) + few_rows(
            u_use, (p_hi[k, here, :], p_lo[k, here, :]))
        return jnp.where(tall % (2 * size) == size, moved, xs)

    state = jnp.zeros((8, width), jnp.float32)
    xs = first_xs
    if ahead:
        known = every
        shown = jnp.zeros((8, group), jnp.float32)
        every = jnp.zeros((8, group), jnp.float32)
        for i in range(chunks):
            c = chunks - 1 - i
            own_p[c * 8:(c + 1) * 8, :] = state
            seen = jnp.where(lane8 // steps == c, known - shown, 0.0)
            every = every + seen
            if c > 0:
                pushed = few_rows(seen, kb)
                if i > 0:
                    pushed = pushed + few_rows(state, tp)
                shown = pushed
                moved = few_rows(seen, (hr_hi[...], hr_lo[...]))
                if i > 0:
                    moved = moved + few_rows(state, top)
                state = moved
            if i < levels:
                xs = expand(levels - 1 - i, xs)
        v_ref[...] = every
        done = min(chunks, levels)
    else:
        state = lax.fori_loop(0, chunks, backward, state)
        done = 0
    for i in range(done, levels):
        xs = expand(levels - 1 - i, xs)
    xs = jnp.where(tall == steps - 1, jnp.broadcast_to(leave, (steps, width)), pltpu.roll(xs, steps - 1, 0))

    v_all = few_rows(v_ref[small, :], (h_hi[here, :], h_lo[here, :]))
    v_own = jnp.where(mine, jnp.broadcast_to(v_all[:1], (steps, group)), 0.0)
    after = own_p[pl.ds(pl.multiple_of(segment * 8, 8), 8), :][:1]
    ps = jnp.where(tall == steps - 1, jnp.broadcast_to(after, (steps, width)), 0.0)
    for k in reversed(range(levels)):
        size = 2**k
        v_use = jnp.where((local > tau) & (local <= tau + size), v_own, 0.0)
        moved = few_rows(pltpu.roll(ps, steps - size, 0), (power_hi[k], power_lo[k])) + few_rows(
            v_use, (r_hi[k, here, :], r_lo[k, here, :]))
        ps = jnp.where((tall + 1) % (2 * size) == size, moved, ps)
    hits = scaled_ref[pl.ds(pl.multiple_of(segment * steps, steps), steps), :]
    change = jnp.sum(jnp.where(local == tau, v_own - u_own, 0.0), axis=1, keepdims=True)
    ss = xs + ps + hits * change
    for i in range(steps):
        filt_ref[i] = xs[i:i + 1]
        smooth_ref[i] = ss[i:i + 1]


def per_device(dynamics, pattern, initial_mean, observed, obs_index, obs_noise):
    rows, width = dynamics.shape
    steps = observed.shape[0]
    members = lax.axis_size("state")
    segments = lax.axis_size("tm")
    total = steps * segments
    levels = steps.bit_length() - 1
    groups = total // LANES
    chunks = segments
    vmem = pl.BlockSpec(memory_space=pltpu.VMEM)
    hbm = pl.BlockSpec(memory_space=pl.ANY)
    dma = pltpu.SemaphoreType.DMA
    full, gathered = pl.pallas_call(
        functools.partial(gather_kernel, members, segments),
        out_shape=(jax.ShapeDtypeStruct((rows * members, width), jnp.float32),
                   jax.ShapeDtypeStruct((total, LANES), jnp.float32)),
        in_specs=[hbm, vmem, vmem, vmem],
        out_specs=(vmem, vmem),
        scratch_shapes=[pltpu.VMEM((LANES, LANES), jnp.float32), pltpu.VMEM((steps, LANES), jnp.float32),
                        dma((PIECES,)), dma((PIECES,)), dma((PIECES,)), dma((PIECES,)), dma, dma,
                        dma((2 * PIECES,)), dma((2 * PIECES,)),
                        dma((segments,)), dma((segments,)), dma],
        compiler_params=pltpu.CompilerParams(collective_id=0, has_side_effects=True),
        name="gather",
    )(dynamics, observed.T, obs_index[None, :], obs_noise[None, :])
    bf, f32 = jnp.bfloat16, jnp.float32
    out = jax.ShapeDtypeStruct((steps, 1, width), f32)
    filtered, smoothed = pl.pallas_call(
        functools.partial(compute_kernel, steps),
        out_shape=(out, out),
        in_specs=[vmem, pl.BlockSpec(memory_space=pltpu.SMEM), vmem, vmem],
        out_specs=(vmem, vmem),
        scratch_shapes=(
            [pltpu.VMEM((levels + 1, width, width), bf)] * 4
            + [pltpu.VMEM((levels + 1, total, width), bf)] * 4
            + [pltpu.VMEM((total, LANES), bf)] * 2
            + [pltpu.VMEM((total, width), f32), pltpu.VMEM((total, LANES), f32)]
            + [pltpu.VMEM((total, width), bf)] * 2
            + [pltpu.VMEM((groups * width, LANES), bf)] * 4
            + [pltpu.VMEM((width, LANES), bf)] * 4
            + [pltpu.VMEM((LANES, LANES), bf)] * 4
            + [pltpu.VMEM((8 * groups, LANES), f32)] * 2
            + [pltpu.VMEM((8 * (chunks + 1), width), f32)] * 3),
        compiler_params=pltpu.CompilerParams(vmem_limit_bytes=56 * 1024 * 1024),
        name="smooth",
    )(full, pattern, initial_mean, gathered)
    return filtered, smoothed


def solution(mesh):
    return jax.shard_map(
        per_device,
        mesh=mesh,
        in_specs=(P("state", None), P(), P(), P("tm", None), P("tm"), P("tm")),
        out_specs=(P("tm", "state", None), P("tm", "state", None)),
        check_vma=False,
    )
```

```python
import functools

import jax
import jax.numpy as jnp
from jax import lax
from jax.experimental import pallas as pl
from jax.experimental.pallas import tpu as pltpu
from jax.sharding import PartitionSpec as P

MESH = pl.DeviceIdType.MESH
PIECES = 4
LANES = 128


def gather_kernel(members, segments, dyn_ref, observed_ref, index_ref, noise_ref, full_ref, obs_ref,
                  raw_ref, packed_ref, x_send, x_recv, y_send, y_recv, c_send, c_recv,
                  f_send, f_recv, o_send, o_recv, own_sem):
    me = lax.axis_index("state")
    seg = lax.axis_index("tm")
    rows = dyn_ref.shape[0]
    sequences, steps = observed_ref.shape
    far = lax.rem(me + members // 2, members)
    near = me + 1 - 2 * lax.rem(me, 2)
    side = lax.rem(seg, 2)
    across = seg + 1 - 2 * side
    barrier = pltpu.get_barrier_semaphore()
    pl.semaphore_signal(barrier, inc=1, device_id={"state": far}, device_id_type=MESH)
    pl.semaphore_signal(barrier, inc=1, device_id={"state": near}, device_id_type=MESH)
    for d in range(1, segments):
        pl.semaphore_signal(barrier, inc=1, device_id={"tm": lax.rem(seg + d, segments)}, device_id_type=MESH)
    pl.semaphore_wait(barrier, segments + 1)

    half = rows // 2
    piece = half // PIECES
    own_start = pl.multiple_of(me * rows, rows)
    far_start = pl.multiple_of(far * rows, rows)
    mine = side * half
    theirs = half - mine
    copies = []
    crossing = []
    swapping = []

    def send(src, dst, sends, recvs, target):
        copy = pltpu.make_async_remote_copy(
            src_ref=src, dst_ref=dst, send_sem=sends, recv_sem=recvs,
            device_id=target, device_id_type=MESH)
        copy.start()
        return copy

    for i in range(PIECES):
        at = pl.multiple_of(mine + i * piece, piece)
        crossing.append(send(dyn_ref.at[pl.ds(at, piece)],
                             full_ref.at[pl.ds(pl.multiple_of(own_start + at, piece), piece)],
                             x_send.at[i], x_recv.at[i], {"state": far}))
    copies.append(send(dyn_ref, full_ref.at[pl.ds(own_start, rows)], c_send, c_recv, {"state": near}))
    raw_ref[...] = jnp.zeros_like(raw_ref)
    raw_ref[:sequences, :steps] = observed_ref[...]
    raw_ref[sequences:sequences + 1, :steps] = index_ref[...].astype(jnp.float32)
    raw_ref[sequences + 1:sequences + 2, :steps] = noise_ref[...]
    packed_ref[...] = raw_ref[...].T[:steps]
    for d in range(1, segments):
        copies.append(send(packed_ref, obs_ref.at[pl.ds(pl.multiple_of(seg * steps, steps), steps)],
                           o_send.at[d], o_recv.at[d], {"tm": lax.rem(seg + d, segments)}))
    own_copy = pltpu.make_async_copy(dyn_ref, full_ref.at[pl.ds(own_start, rows)], own_sem)
    own_copy.start()
    obs_ref[pl.ds(pl.multiple_of(seg * steps, steps), steps)] = packed_ref[...]
    for i in range(PIECES):
        crossing[i].wait_recv()
        spot = pl.ds(pl.multiple_of(far_start + mine + i * piece, piece), piece)
        swapping.append(send(full_ref.at[spot], full_ref.at[spot], y_send.at[i], y_recv.at[i], {"tm": across}))
        copies.append(send(full_ref.at[spot], full_ref.at[spot], f_send.at[i], f_recv.at[i], {"state": near}))
    for i in range(PIECES):
        swapping[i].wait_recv()
        spot = pl.ds(pl.multiple_of(far_start + theirs + i * piece, piece), piece)
        copies.append(send(full_ref.at[spot], full_ref.at[spot], f_send.at[PIECES + i],
                           f_recv.at[PIECES + i], {"state": near}))
    own_copy.wait()
    for copy in crossing + swapping:
        copy.wait_send()
    for copy in copies:
        copy.wait()


def halves(value):
    high = value.astype(jnp.bfloat16)
    low = (value - high.astype(jnp.float32)).astype(jnp.bfloat16)
    return high, low


def contract(left, right, dims):
    return lax.dot_general(left, right, (dims, ((), ())), preferred_element_type=jnp.float32)


def multiply(left, right, dims=((1,), (0,))):
    stacked = jnp.concatenate([left[0], left[1], left[0]], axis=1)
    other = jnp.concatenate([right[1], right[0], right[0]], axis=dims[1][0])
    return contract(stacked, other, dims)


def stacked_left(pair):
    return jnp.concatenate([pair[0], pair[1], pair[0]], axis=1)


def keep_rows(ref, index, start, pair, times):
    size = pair[0].shape[0]
    for i, part in enumerate((pair[1], pair[0], pair[0])[:times]):
        ref[index + (pl.ds(pl.multiple_of(start + i * size, size), size), slice(None))] = part


TRANS = ((1,), (1,))


def few_rows(left, right):
    count = left.shape[0]
    high = left.astype(jnp.bfloat16).astype(jnp.float32)
    both = jnp.concatenate([high, left - high], axis=0).astype(jnp.bfloat16)
    total = contract(jnp.concatenate([both, both], axis=1), right, ((1,), (0,)))
    return total[:count] + total[count:]


def compute_kernel(steps, full_ref, pattern_ref, mean_ref, obs_ref, filt_ref, smooth_ref,
                   power_left, power, power_t, r_rows, p_rows, h_rows, hr_rows, hr_t, p_t,
                   scaled_ref, obs_in_ref, u_ref, v_ref, x_ref, own_x, own_p):
    width = full_ref.shape[1]
    total = obs_ref.shape[0]
    blocks = pattern_ref.shape[0]
    span = width // blocks
    group = LANES
    groups = total // group
    chunks = total // steps
    per_group = group // steps
    levels = steps.bit_length() - 1
    sequences = mean_ref.shape[0]
    member = lax.axis_index("state")
    segment = lax.axis_index("tm")

    for i in range(blocks):
        for j in range(blocks):
            tile = full_ref[i * span:(i + 1) * span, j * span:(j + 1) * span]
            if i != j:
                tile = tile * jnp.maximum(pattern_ref[i, j], 0).astype(jnp.float32)
            down, over = slice(i * span, (i + 1) * span), slice(j * span, (j + 1) * span)
            hi, lo = halves(tile)
            turned_hi, turned_lo = halves(tile.T)
            for n, (part, turned) in enumerate(((lo, turned_lo), (hi, turned_hi), (hi, turned_hi))):
                power[0, n * width + i * span:n * width + (i + 1) * span, over] = part
                power_t[0, n * width + j * span:n * width + (j + 1) * span, down] = turned
            for n, part in enumerate((hi, lo, hi)):
                power_left[0, down, n * width + j * span:n * width + (j + 1) * span] = part

    def advance(k):
        square = contract(power_left[k], power[k], ((1,), (0,)))
        hi, lo = halves(square)
        keep_rows(power, (k + 1,), 0, (hi, lo), 3)
        keep_rows(power_t, (k + 1,), 0, halves(square.T), 3)
        if k + 1 < levels:
            for n, part in enumerate((hi, lo, hi)):
                power_left[k + 1, :, n * width:(n + 1) * width] = part

    if groups > 1:
        for k in range(levels):
            advance(k)

    row = lax.broadcasted_iota(jnp.int32, (group, group), 0)
    col = lax.broadcasted_iota(jnp.int32, (group, group), 1)
    wide = lax.broadcasted_iota(jnp.int32, (group, width), 1)
    row_wide = lax.broadcasted_iota(jnp.int32, (group, width), 0)

    def prepare(g):
        here = pl.ds(pl.multiple_of(g * group, group), group)
        packed = obs_ref[here, :]
        index = jnp.sum(jnp.where(col == sequences, packed, 0.0), axis=1, keepdims=True).astype(jnp.int32)
        noise = jnp.sum(jnp.where(col == sequences + 1, packed, 0.0), axis=1, keepdims=True)
        observed = jnp.sum(jnp.where(col == member, packed, 0.0), axis=1, keepdims=True)
        root = jnp.sqrt(1.0 / (1.0 + noise))
        scaled = jnp.where(wide == index, root, 0.0)
        scaled_ref[here, :] = scaled
        p_now = scaled
        two = 2 * group * g
        r_now = contract(stacked_left(halves(scaled)), power[0], ((1,), (0,)))
        inverse = jnp.where(row == col, 1.0, 0.0)
        for k in range(levels):
            if groups == 1:
                advance(k)
            r_pair = halves(r_now)
            p_pair = halves(p_now)
            keep_rows(r_rows, (k,), two, r_pair, 2)
            keep_rows(p_rows, (k,), two, p_pair, 2)
            gram = multiply(r_pair, p_pair, TRANS)
            size = 2**k
            sibling = ((row // (2 * size)) == (col // (2 * size))) & ((row // size) == (col // size) + 1)
            gram = jnp.where(sibling, gram, 0.0)
            if k == 0:
                inverse = inverse - gram
            else:
                pair = halves(inverse)
                inverse = inverse - multiply(halves(multiply(pair, halves(gram))), pair)
            set_bit = ((row_wide // size) % 2) == 1
            r_now = jnp.where(set_bit, contract(stacked_left(r_pair), power[k], ((1,), (0,))), r_now)
            p_now = jnp.where(set_bit, p_now, contract(stacked_left(p_pair), power_t[k], ((1,), (0,))))
        r_pair = halves(r_now)
        keep_rows(r_rows, (levels,), two, r_pair, 2)
        keep_rows(p_rows, (levels,), two, halves(p_now), 2)
        keep_rows(p_t, (), 2 * width * g, halves(p_now.T), 2)
        pair = halves(inverse)
        keep_rows(h_rows, (), two, pair, 2)
        response = multiply(pair, r_pair)
        keep_rows(hr_rows, (), two, halves(response), 2)
        keep_rows(hr_t, (), 2 * width * g, halves(response.T), 2)
        source = multiply(pair, halves(jnp.where(col == member, observed * root, 0.0)))
        obs_in_ref[here, :] = jnp.broadcast_to(
            jnp.sum(source.T, axis=0, keepdims=True), (group, group))

    if groups == 1:
        prepare(0)
    else:
        lax.fori_loop(0, groups, lambda g, c: (prepare(g), c)[1], 0)

    lane8 = lax.broadcasted_iota(jnp.int32, (8, group), 1)
    u_ref[...] = jnp.zeros_like(u_ref)
    v_ref[...] = jnp.zeros_like(v_ref)
    top, top_t = power[levels, :2 * width], power_t[levels, :2 * width]

    def here_of(c):
        g = c // per_group
        return (pl.ds(pl.multiple_of(g * 2 * group, 2 * group), 2 * group),
                pl.ds(pl.multiple_of(g * 8, 8), 8), c % per_group,
                pl.ds(pl.multiple_of(g * 2 * width, 2 * width), 2 * width))

    def forward(c, state):
        here, small, spot, tall_here = here_of(c)
        x_ref[pl.ds(pl.multiple_of(c * 8, 8), 8), :] = state
        first = pl.ds(pl.multiple_of((c // per_group) * group, group), 8)
        drive = obs_in_ref[first, :] - few_rows(state, hr_t[tall_here, :])
        drive = jnp.where(lane8 // steps == spot, drive, 0.0)
        u_ref[small, :] = u_ref[small, :] + drive
        return few_rows(state, top_t) + few_rows(drive, p_rows[levels, here, :])

    mean = jnp.sum(
        jnp.where(lax.broadcasted_iota(jnp.int32, mean_ref.shape, 0) == member, mean_ref[...], 0.0),
        axis=0, keepdims=True)
    state = jnp.broadcast_to(mean, (8, width))
    if chunks <= 8:
        for c in range(chunks):
            state = forward(c, state)
    else:
        state = lax.fori_loop(0, chunks, forward, state)
    x_ref[chunks * 8:(chunks + 1) * 8, :] = state

    def backward(i, state):
        c = chunks - 1 - i
        here, small, spot, tall_here = here_of(c)
        own_p[pl.ds(pl.multiple_of(c * 8, 8), 8), :] = state
        seen = u_ref[small, :] - few_rows(state, p_t[tall_here, :])
        seen = jnp.where(lane8 // steps == spot, seen, 0.0)
        v_ref[small, :] = v_ref[small, :] + seen
        return few_rows(state, top) + few_rows(seen, hr_rows[here, :])

    here, small, spot, _ = here_of(segment)
    lane = lax.broadcasted_iota(jnp.int32, (steps, group), 1)
    tau = lax.broadcasted_iota(jnp.int32, (steps, group), 0)
    tall = lax.broadcasted_iota(jnp.int32, (steps, width), 0)
    local = lane - spot * steps
    mine = (local >= 0) & (local < steps)
    u_own = jnp.where(mine, jnp.broadcast_to(u_ref[small, :][:1], (steps, group)), 0.0)
    enter = x_ref[pl.ds(pl.multiple_of(segment * 8, 8), 8), :][:1]
    leave = x_ref[pl.ds(pl.multiple_of((segment + 1) * 8, 8), 8), :][:1]
    first_xs = jnp.where(tall == 0, jnp.broadcast_to(enter, (steps, width)), 0.0)

    def expand(k, xs):
        size = 2**k
        u_use = jnp.where((local >= tau - size) & (local < tau), u_own, 0.0)
        moved = few_rows(pltpu.roll(xs, size, 0), power_t[k, :2 * width]) + few_rows(
            u_use, p_rows[k, here, :])
        return jnp.where(tall % (2 * size) == size, moved, xs)

    state = jnp.zeros((8, width), jnp.float32)
    xs = first_xs
    if chunks <= 8:
        for i in range(chunks):
            state = backward(i, state)
            if i < levels:
                xs = expand(levels - 1 - i, xs)
        done = min(chunks, levels)
    else:
        state = lax.fori_loop(0, chunks, backward, state)
        done = 0
    for i in range(done, levels):
        xs = expand(levels - 1 - i, xs)
    xs = jnp.where(tall == steps - 1, jnp.broadcast_to(leave, (steps, width)), pltpu.roll(xs, steps - 1, 0))

    v_all = few_rows(v_ref[small, :], h_rows[here, :])
    v_own = jnp.where(mine, jnp.broadcast_to(v_all[:1], (steps, group)), 0.0)
    after = own_p[pl.ds(pl.multiple_of(segment * 8, 8), 8), :][:1]
    ps = jnp.where(tall == steps - 1, jnp.broadcast_to(after, (steps, width)), 0.0)
    for k in reversed(range(levels)):
        size = 2**k
        v_use = jnp.where((local > tau) & (local <= tau + size), v_own, 0.0)
        moved = few_rows(pltpu.roll(ps, steps - size, 0), power[k, :2 * width]) + few_rows(
            v_use, r_rows[k, here, :])
        ps = jnp.where((tall + 1) % (2 * size) == size, moved, ps)
    hits = scaled_ref[pl.ds(pl.multiple_of(segment * steps, steps), steps), :]
    change = jnp.sum(jnp.where(local == tau, v_own - u_own, 0.0), axis=1, keepdims=True)
    ss = xs + ps + hits * change
    for i in range(steps):
        filt_ref[i] = xs[i:i + 1]
        smooth_ref[i] = ss[i:i + 1]


def per_device(dynamics, pattern, initial_mean, observed, obs_index, obs_noise):
    rows, width = dynamics.shape
    steps = observed.shape[0]
    members = lax.axis_size("state")
    segments = lax.axis_size("tm")
    total = steps * segments
    levels = steps.bit_length() - 1
    groups = total // LANES
    chunks = segments
    vmem = pl.BlockSpec(memory_space=pltpu.VMEM)
    hbm = pl.BlockSpec(memory_space=pl.ANY)
    dma = pltpu.SemaphoreType.DMA
    full, gathered = pl.pallas_call(
        functools.partial(gather_kernel, members, segments),
        out_shape=(jax.ShapeDtypeStruct((rows * members, width), jnp.float32),
                   jax.ShapeDtypeStruct((total, LANES), jnp.float32)),
        in_specs=[hbm, vmem, vmem, vmem],
        out_specs=(vmem, vmem),
        scratch_shapes=[pltpu.VMEM((LANES, LANES), jnp.float32), pltpu.VMEM((steps, LANES), jnp.float32),
                        dma((PIECES,)), dma((PIECES,)), dma((PIECES,)), dma((PIECES,)), dma, dma,
                        dma((2 * PIECES,)), dma((2 * PIECES,)),
                        dma((segments,)), dma((segments,)), dma],
        compiler_params=pltpu.CompilerParams(collective_id=0, has_side_effects=True),
        name="gather",
    )(dynamics, observed.T, obs_index[None, :], obs_noise[None, :])
    bf, f32 = jnp.bfloat16, jnp.float32
    out = jax.ShapeDtypeStruct((steps, 1, width), f32)
    filtered, smoothed = pl.pallas_call(
        functools.partial(compute_kernel, steps),
        out_shape=(out, out),
        in_specs=[vmem, pl.BlockSpec(memory_space=pltpu.SMEM), vmem, vmem],
        out_specs=(vmem, vmem),
        scratch_shapes=(
            [pltpu.VMEM((levels, width, 3 * width), bf)]
            + [pltpu.VMEM((levels + 1, 3 * width, width), bf)] * 2
            + [pltpu.VMEM((levels + 1, 2 * total, width), bf)] * 2
            + [pltpu.VMEM((2 * total, LANES), bf), pltpu.VMEM((2 * total, width), bf)]
            + [pltpu.VMEM((2 * groups * width, LANES), bf)] * 2
            + [pltpu.VMEM((total, width), f32), pltpu.VMEM((total, LANES), f32)]
            + [pltpu.VMEM((8 * groups, LANES), f32)] * 2
            + [pltpu.VMEM((8 * (chunks + 1), width), f32)] * 3),
        compiler_params=pltpu.CompilerParams(vmem_limit_bytes=56 * 1024 * 1024),
        name="smooth",
    )(full, pattern, initial_mean, gathered)
    return filtered, smoothed


def solution(mesh):
    return jax.shard_map(
        per_device,
        mesh=mesh,
        in_specs=(P("state", None), P(), P(), P("tm", None), P("tm"), P("tm")),
        out_specs=(P("tm", "state", None), P("tm", "state", None)),
        check_vma=False,
    )
```

```python
import functools

import jax
import jax.numpy as jnp
from jax import lax
from jax.experimental import pallas as pl
from jax.experimental.pallas import tpu as pltpu
from jax.sharding import PartitionSpec as P

MESH = pl.DeviceIdType.MESH
PIECES = 4
LANES = 128


def gather_kernel(members, segments, dyn_ref, observed_ref, index_ref, noise_ref, full_ref, obs_ref,
                  raw_ref, packed_ref, x_send, x_recv, y_send, y_recv, c_send, c_recv,
                  f_send, f_recv, o_send, o_recv, own_sem):
    me = lax.axis_index("state")
    seg = lax.axis_index("tm")
    rows = dyn_ref.shape[0]
    sequences, steps = observed_ref.shape
    far = lax.rem(me + members // 2, members)
    near = me + 1 - 2 * lax.rem(me, 2)
    side = lax.rem(seg, 2)
    across = seg + 1 - 2 * side
    barrier = pltpu.get_barrier_semaphore()
    pl.semaphore_signal(barrier, inc=1, device_id={"state": far}, device_id_type=MESH)
    pl.semaphore_signal(barrier, inc=1, device_id={"state": near}, device_id_type=MESH)
    for d in range(1, segments):
        pl.semaphore_signal(barrier, inc=1, device_id={"tm": lax.rem(seg + d, segments)}, device_id_type=MESH)
    pl.semaphore_wait(barrier, segments + 1)

    half = rows // 2
    piece = half // PIECES
    own_start = pl.multiple_of(me * rows, rows)
    far_start = pl.multiple_of(far * rows, rows)
    mine = side * half
    theirs = half - mine
    copies = []
    crossing = []
    swapping = []

    def send(src, dst, sends, recvs, target):
        copy = pltpu.make_async_remote_copy(
            src_ref=src, dst_ref=dst, send_sem=sends, recv_sem=recvs,
            device_id=target, device_id_type=MESH)
        copy.start()
        return copy

    for i in range(PIECES):
        at = pl.multiple_of(mine + i * piece, piece)
        crossing.append(send(dyn_ref.at[pl.ds(at, piece)],
                             full_ref.at[pl.ds(pl.multiple_of(own_start + at, piece), piece)],
                             x_send.at[i], x_recv.at[i], {"state": far}))
    copies.append(send(dyn_ref, full_ref.at[pl.ds(own_start, rows)], c_send, c_recv, {"state": near}))
    raw_ref[...] = jnp.zeros_like(raw_ref)
    raw_ref[:sequences, :steps] = observed_ref[...]
    raw_ref[sequences:sequences + 1, :steps] = index_ref[...].astype(jnp.float32)
    raw_ref[sequences + 1:sequences + 2, :steps] = noise_ref[...]
    packed_ref[...] = raw_ref[...].T[:steps]
    for d in range(1, segments):
        copies.append(send(packed_ref, obs_ref.at[pl.ds(pl.multiple_of(seg * steps, steps), steps)],
                           o_send.at[d], o_recv.at[d], {"tm": lax.rem(seg + d, segments)}))
    own_copy = pltpu.make_async_copy(dyn_ref, full_ref.at[pl.ds(own_start, rows)], own_sem)
    own_copy.start()
    obs_ref[pl.ds(pl.multiple_of(seg * steps, steps), steps)] = packed_ref[...]
    for i in range(PIECES):
        crossing[i].wait_recv()
        spot = pl.ds(pl.multiple_of(far_start + mine + i * piece, piece), piece)
        swapping.append(send(full_ref.at[spot], full_ref.at[spot], y_send.at[i], y_recv.at[i], {"tm": across}))
        copies.append(send(full_ref.at[spot], full_ref.at[spot], f_send.at[i], f_recv.at[i], {"state": near}))
    for i in range(PIECES):
        swapping[i].wait_recv()
        spot = pl.ds(pl.multiple_of(far_start + theirs + i * piece, piece), piece)
        copies.append(send(full_ref.at[spot], full_ref.at[spot], f_send.at[PIECES + i],
                           f_recv.at[PIECES + i], {"state": near}))
    own_copy.wait()
    for copy in crossing + swapping:
        copy.wait_send()
    for copy in copies:
        copy.wait()


def halves(value):
    high = value.astype(jnp.bfloat16)
    low = (value - high.astype(jnp.float32)).astype(jnp.bfloat16)
    return high, low


def contract(left, right, dims):
    return lax.dot_general(left, right, (dims, ((), ())), preferred_element_type=jnp.float32)


def multiply(left, right, dims=((1,), (0,))):
    stacked = jnp.concatenate([left[0], left[1], left[0]], axis=1)
    other = jnp.concatenate([right[1], right[0], right[0]], axis=dims[1][0])
    return contract(stacked, other, dims)


TRANS = ((1,), (1,))


def few_rows(left, right, dims=((1,), (0,))):
    count = left.shape[0]
    high = left.astype(jnp.bfloat16).astype(jnp.float32)
    both = jnp.concatenate([high, left - high], axis=0).astype(jnp.bfloat16)
    total = contract(jnp.concatenate([both, both], axis=1), jnp.concatenate([right[1], right[0]], axis=dims[1][0]), dims)
    return total[:count] + total[count:]


def compute_kernel(steps, full_ref, pattern_ref, mean_ref, obs_ref, filt_ref, smooth_ref,
                   power_hi, power_lo, powert_hi, powert_lo, r_hi, r_lo, p_hi, p_lo, h_hi, h_lo,
                   scaled_ref, obs_in_ref, hr_hi, hr_lo, hrt_hi, hrt_lo, pt_hi, pt_lo, u_ref, v_ref, x_ref, own_x, own_p):
    width = full_ref.shape[1]
    total = obs_ref.shape[0]
    blocks = pattern_ref.shape[0]
    span = width // blocks
    group = LANES
    groups = total // group
    chunks = total // steps
    per_group = group // steps
    levels = steps.bit_length() - 1
    sequences = mean_ref.shape[0]
    member = lax.axis_index("state")
    segment = lax.axis_index("tm")

    for i in range(blocks):
        for j in range(blocks):
            tile = full_ref[i * span:(i + 1) * span, j * span:(j + 1) * span]
            if i != j:
                tile = tile * jnp.maximum(pattern_ref[i, j], 0).astype(jnp.float32)
            down, over = slice(i * span, (i + 1) * span), slice(j * span, (j + 1) * span)
            power_hi[0, down, over], power_lo[0, down, over] = halves(tile)
            powert_hi[0, over, down], powert_lo[0, over, down] = halves(tile.T)

    def advance(k):
        square = multiply((power_hi[k], power_lo[k]), (power_hi[k], power_lo[k]))
        power_hi[k + 1], power_lo[k + 1] = halves(square)
        powert_hi[k + 1], powert_lo[k + 1] = halves(square.T)

    if groups > 1:
        for k in range(levels):
            advance(k)

    row = lax.broadcasted_iota(jnp.int32, (group, group), 0)
    col = lax.broadcasted_iota(jnp.int32, (group, group), 1)
    wide = lax.broadcasted_iota(jnp.int32, (group, width), 1)
    row_wide = lax.broadcasted_iota(jnp.int32, (group, width), 0)

    def prepare(g):
        here = pl.ds(pl.multiple_of(g * group, group), group)
        packed = obs_ref[here, :]
        index = jnp.sum(jnp.where(col == sequences, packed, 0.0), axis=1, keepdims=True).astype(jnp.int32)
        noise = jnp.sum(jnp.where(col == sequences + 1, packed, 0.0), axis=1, keepdims=True)
        observed = jnp.sum(jnp.where(col == member, packed, 0.0), axis=1, keepdims=True)
        root = jnp.sqrt(1.0 / (1.0 + noise))
        scaled = jnp.where(wide == index, root, 0.0)
        scaled_ref[here, :] = scaled
        p_now = scaled
        r_now = multiply(halves(scaled), (power_hi[0], power_lo[0]))
        inverse = jnp.where(row == col, 1.0, 0.0)
        for k in range(levels):
            if groups == 1:
                advance(k)
            r_pair = halves(r_now)
            p_pair = halves(p_now)
            r_hi[k, here, :], r_lo[k, here, :] = r_pair
            p_hi[k, here, :], p_lo[k, here, :] = p_pair
            gram = multiply(r_pair, p_pair, TRANS)
            size = 2**k
            sibling = ((row // (2 * size)) == (col // (2 * size))) & ((row // size) == (col // size) + 1)
            gram = jnp.where(sibling, gram, 0.0)
            if k == 0:
                inverse = inverse - gram
            else:
                pair = halves(inverse)
                inverse = inverse - multiply(halves(multiply(pair, halves(gram))), pair)
            set_bit = ((row_wide // size) % 2) == 1
            r_now = jnp.where(set_bit, multiply(r_pair, (power_hi[k], power_lo[k])), r_now)
            p_now = jnp.where(set_bit, p_now, multiply(p_pair, (powert_hi[k], powert_lo[k])))
        r_pair = halves(r_now)
        r_hi[levels, here, :], r_lo[levels, here, :] = r_pair
        p_hi[levels, here, :], p_lo[levels, here, :] = halves(p_now)
        tall_here = pl.ds(pl.multiple_of(g * width, width), width)
        pt_hi[tall_here, :], pt_lo[tall_here, :] = halves(p_now.T)
        pair = halves(inverse)
        h_hi[here, :], h_lo[here, :] = pair
        response = multiply(pair, r_pair)
        hr_hi[here, :], hr_lo[here, :] = halves(response)
        hrt_hi[tall_here, :], hrt_lo[tall_here, :] = halves(response.T)
        source = multiply(pair, halves(jnp.where(col == member, observed * root, 0.0)))
        obs_in_ref[here, :] = jnp.broadcast_to(
            jnp.sum(source.T, axis=0, keepdims=True), (group, group))

    if groups == 1:
        prepare(0)
    else:
        lax.fori_loop(0, groups, lambda g, c: (prepare(g), c)[1], 0)

    lane8 = lax.broadcasted_iota(jnp.int32, (8, group), 1)
    u_ref[...] = jnp.zeros_like(u_ref)
    v_ref[...] = jnp.zeros_like(v_ref)
    top = (power_hi[levels], power_lo[levels])
    top_t = (powert_hi[levels], powert_lo[levels])

    def here_of(c):
        g = c // per_group
        return pl.ds(pl.multiple_of(g * group, group), group), pl.ds(pl.multiple_of(g * 8, 8), 8), c % per_group

    def forward(c, state):
        here, small, spot = here_of(c)
        x_ref[pl.ds(pl.multiple_of(c * 8, 8), 8), :] = state
        first = pl.ds(pl.multiple_of((c // per_group) * group, group), 8)
        tall_here = pl.ds(pl.multiple_of((c // per_group) * width, width), width)
        drive = obs_in_ref[first, :] - few_rows(state, (hrt_hi[tall_here, :], hrt_lo[tall_here, :]))
        drive = jnp.where(lane8 // steps == spot, drive, 0.0)
        u_ref[small, :] = u_ref[small, :] + drive
        return few_rows(state, top_t) + few_rows(drive, (p_hi[levels, here, :], p_lo[levels, here, :]))

    mean = jnp.sum(
        jnp.where(lax.broadcasted_iota(jnp.int32, mean_ref.shape, 0) == member, mean_ref[...], 0.0),
        axis=0, keepdims=True)
    state = jnp.broadcast_to(mean, (8, width))
    if chunks <= 8:
        for c in range(chunks):
            state = forward(c, state)
    else:
        state = lax.fori_loop(0, chunks, forward, state)
    x_ref[chunks * 8:(chunks + 1) * 8, :] = state

    def backward(i, state):
        c = chunks - 1 - i
        here, small, spot = here_of(c)
        own_p[pl.ds(pl.multiple_of(c * 8, 8), 8), :] = state
        tall_here = pl.ds(pl.multiple_of((c // per_group) * width, width), width)
        seen = u_ref[small, :] - few_rows(state, (pt_hi[tall_here, :], pt_lo[tall_here, :]))
        seen = jnp.where(lane8 // steps == spot, seen, 0.0)
        v_ref[small, :] = v_ref[small, :] + seen
        return few_rows(state, top) + few_rows(seen, (hr_hi[here, :], hr_lo[here, :]))

    here, small, spot = here_of(segment)
    lane = lax.broadcasted_iota(jnp.int32, (steps, group), 1)
    tau = lax.broadcasted_iota(jnp.int32, (steps, group), 0)
    tall = lax.broadcasted_iota(jnp.int32, (steps, width), 0)
    local = lane - spot * steps
    mine = (local >= 0) & (local < steps)
    u_own = jnp.where(mine, jnp.broadcast_to(u_ref[small, :][:1], (steps, group)), 0.0)
    enter = x_ref[pl.ds(pl.multiple_of(segment * 8, 8), 8), :][:1]
    leave = x_ref[pl.ds(pl.multiple_of((segment + 1) * 8, 8), 8), :][:1]
    first_xs = jnp.where(tall == 0, jnp.broadcast_to(enter, (steps, width)), 0.0)

    def expand(k, xs):
        size = 2**k
        u_use = jnp.where((local >= tau - size) & (local < tau), u_own, 0.0)
        moved = few_rows(pltpu.roll(xs, size, 0), (powert_hi[k], powert_lo[k])) + few_rows(
            u_use, (p_hi[k, here, :], p_lo[k, here, :]))
        return jnp.where(tall % (2 * size) == size, moved, xs)

    state = jnp.zeros((8, width), jnp.float32)
    xs = first_xs
    if chunks <= 8:
        for i in range(chunks):
            state = backward(i, state)
            if i < levels:
                xs = expand(levels - 1 - i, xs)
        done = min(chunks, levels)
    else:
        state = lax.fori_loop(0, chunks, backward, state)
        done = 0
    for i in range(done, levels):
        xs = expand(levels - 1 - i, xs)
    xs = jnp.where(tall == steps - 1, jnp.broadcast_to(leave, (steps, width)), pltpu.roll(xs, steps - 1, 0))

    v_all = few_rows(v_ref[small, :], (h_hi[here, :], h_lo[here, :]))
    v_own = jnp.where(mine, jnp.broadcast_to(v_all[:1], (steps, group)), 0.0)
    after = own_p[pl.ds(pl.multiple_of(segment * 8, 8), 8), :][:1]
    ps = jnp.where(tall == steps - 1, jnp.broadcast_to(after, (steps, width)), 0.0)
    for k in reversed(range(levels)):
        size = 2**k
        v_use = jnp.where((local > tau) & (local <= tau + size), v_own, 0.0)
        moved = few_rows(pltpu.roll(ps, steps - size, 0), (power_hi[k], power_lo[k])) + few_rows(
            v_use, (r_hi[k, here, :], r_lo[k, here, :]))
        ps = jnp.where((tall + 1) % (2 * size) == size, moved, ps)
    hits = scaled_ref[pl.ds(pl.multiple_of(segment * steps, steps), steps), :]
    change = jnp.sum(jnp.where(local == tau, v_own - u_own, 0.0), axis=1, keepdims=True)
    ss = xs + ps + hits * change
    for i in range(steps):
        filt_ref[i] = xs[i:i + 1]
        smooth_ref[i] = ss[i:i + 1]


def per_device(dynamics, pattern, initial_mean, observed, obs_index, obs_noise):
    rows, width = dynamics.shape
    steps = observed.shape[0]
    members = lax.axis_size("state")
    segments = lax.axis_size("tm")
    total = steps * segments
    levels = steps.bit_length() - 1
    groups = total // LANES
    chunks = segments
    vmem = pl.BlockSpec(memory_space=pltpu.VMEM)
    hbm = pl.BlockSpec(memory_space=pl.ANY)
    dma = pltpu.SemaphoreType.DMA
    full, gathered = pl.pallas_call(
        functools.partial(gather_kernel, members, segments),
        out_shape=(jax.ShapeDtypeStruct((rows * members, width), jnp.float32),
                   jax.ShapeDtypeStruct((total, LANES), jnp.float32)),
        in_specs=[hbm, vmem, vmem, vmem],
        out_specs=(vmem, vmem),
        scratch_shapes=[pltpu.VMEM((LANES, LANES), jnp.float32), pltpu.VMEM((steps, LANES), jnp.float32),
                        dma((PIECES,)), dma((PIECES,)), dma((PIECES,)), dma((PIECES,)), dma, dma,
                        dma((2 * PIECES,)), dma((2 * PIECES,)),
                        dma((segments,)), dma((segments,)), dma],
        compiler_params=pltpu.CompilerParams(collective_id=0, has_side_effects=True,
                                             vmem_limit_bytes=8 * 1024 * 1024),
        name="gather",
    )(dynamics, observed.T, obs_index[None, :], obs_noise[None, :])
    bf, f32 = jnp.bfloat16, jnp.float32
    out = jax.ShapeDtypeStruct((steps, 1, width), f32)
    filtered, smoothed = pl.pallas_call(
        functools.partial(compute_kernel, steps),
        out_shape=(out, out),
        in_specs=[vmem, pl.BlockSpec(memory_space=pltpu.SMEM), vmem, vmem],
        out_specs=(vmem, vmem),
        scratch_shapes=(
            [pltpu.VMEM((levels + 1, width, width), bf)] * 4
            + [pltpu.VMEM((levels + 1, total, width), bf)] * 4
            + [pltpu.VMEM((total, LANES), bf)] * 2
            + [pltpu.VMEM((total, width), f32), pltpu.VMEM((total, LANES), f32)]
            + [pltpu.VMEM((total, width), bf)] * 2
            + [pltpu.VMEM((groups * width, LANES), bf)] * 4
            + [pltpu.VMEM((8 * groups, LANES), f32)] * 2
            + [pltpu.VMEM((8 * (chunks + 1), width), f32)] * 3),
        compiler_params=pltpu.CompilerParams(vmem_limit_bytes=(20 + 12 * groups) * 1024 * 1024 if groups == 1 else 56 * 1024 * 1024),
        name="smooth",
    )(full, pattern, initial_mean, gathered)
    return filtered, smoothed


def solution(mesh):
    return jax.shard_map(
        per_device,
        mesh=mesh,
        in_specs=(P("state", None), P(), P(), P("tm", None), P("tm"), P("tm")),
        out_specs=(P("tm", "state", None), P("tm", "state", None)),
        check_vma=False,
    )
```
